32 devices in a mesh: blk: 8 (over z, y), quarter: 4 (over x, core).
Axes of the slice: x: 2, y: 2, z: 4, core: 2. Of those that a mesh axis runs over, the one named last changes fastest.
Arguments:
- start: float32 [2048, 2, 2048], P(('blk', 'quarter')), may hold values from -6 to 6
- observed: float32 [4, 16, 4096], P(None, 'blk', 'quarter'), may hold values from -6 to 6
- coverage: int32 [4, 16, 4096], P(None, 'blk', 'quarter'), may hold values from 0 to 4
- class_weight: float32 [4, 4], replicated, may hold values from 0.25 to 4
- degree_gain: float32 [4, 2048], replicated, may hold values from 0.5 to 2
- legendre: bfloat16 [2048, 8, 2048], P(('blk', 'quarter')), as said below
- order_table: int32 [2048], replicated, may hold values from 0 to 2047, as said below
Outputs:
- solution: float32 [2048, 2, 2048], P(('blk', 'quarter'))
- gradient: float32 [2048, 2, 2048], P(('blk', 'quarter'))
The draws below stay inside these ranges and needn't reach their ends.
Inputs may be any that keep to these rules, and one draw needn't show every extreme that they name: `order_table`: slots 2i and 2i + 1 hold the orders i and 2047 - i, one each, for every i below 1024. legendre[s, j, l] is zero wherever the degree l is below the order of slot s.
All inputs are finite; a program needn't handle non-finite values.
Results may differ from the reference program's by a relative error of at most 0.02.
Values may be sent and summed in bfloat16 or wider, within the bound.
A program may use at most 128 MiB of HBM per device.

```python
import math
import jax
import jax.numpy as jnp
from jax import lax

NORD = 2048
DEG = 2048
NLON = 4096
FUNC = 4
CLASSES = 4
ITERS = 2
RH = 8
CYCLES = 16


def pair_orders(key):
    flips = jax.random.randint(key, (NORD // 2,), 0, 2)
    lower = jnp.arange(NORD // 2, dtype=jnp.int32)
    upper = NORD - 1 - lower
    first_order = jnp.where(flips == 1, upper, lower)
    second_order = jnp.where(flips == 1, lower, upper)
    return jnp.stack([first_order, second_order], 1).reshape(NORD).astype(jnp.int32)


def draw_order_table(key, part):
    orders = pair_orders(key)
    return orders


def draw_legendre(key, part):
    orders = pair_orders(key)
    key = jax.random.fold_in(key, 2)
    degrees = jnp.arange(DEG, dtype=jnp.int32)
    live = degrees[None, None, :] >= orders[:, None, None]
    values = jax.random.normal(key, (NORD, RH, DEG), jnp.float32)
    values = values * DEG ** (-0.5)
    return jnp.where(live, values, 0.0).astype(jnp.bfloat16)


def place_ends(values, rng, least, top_value):
    dims = values.shape
    place = [jax.random.randint(jax.random.fold_in(rng, axis), (), 0, dims[axis]) for axis in range(len(dims))]
    values = values.at[tuple(place)].set(least)
    longest = dims.index(max(dims))
    place[longest] = (place[longest] + 1) % dims[longest]
    return values.at[tuple(place)].set(top_value)


def block_levels(stream_key, shape, cuts, smallest, high):
    factor_of, own = 1.0, jax.random.fold_in(stream_key, 6)
    for dim, parts in cuts:
        draws = jnp.exp(jax.random.uniform(jax.random.fold_in(own, dim), (parts,), jnp.float32, smallest / len(cuts), high / len(cuts)))
        factor_of = factor_of * jnp.repeat(draws, shape[dim] // parts).reshape([-1 if axis == dim else 1 for axis in range(len(shape))])
    return factor_of


def normal_values(rng, shape, scale, reach, cuts=(), held_as=jnp.bfloat16):
    result = scale * jax.random.normal(rng, shape, jnp.float32)
    if cuts:
        result = result * block_levels(rng, shape, cuts, -0.22, 0.18)
    return jnp.clip(result, -reach, reach).astype(held_as)


def setup_inputs(seed: int = 0) -> dict:
    streams_of = jax.random.split(jax.random.key(seed), 8)
    return {
        "start": normal_values(streams_of[0], (NORD, 2, DEG), 1.0, 6.0, ((0, 32),), jnp.float32),
        "observed": normal_values(streams_of[1], (FUNC, CYCLES, NLON), 1.0, 6.0, ((1, 8), (2, 4)), jnp.float32),
        "coverage": place_ends(jax.random.randint(streams_of[2], (FUNC, CYCLES, NLON), 0, CLASSES + 1), jax.random.fold_in(streams_of[2], 1), 0, CLASSES).astype(jnp.int32),
        "class_weight": jnp.clip(jnp.exp(jax.random.uniform(streams_of[3], (FUNC, CLASSES), jnp.float32, math.log(0.25), math.log(4.0))), 0.25, 4.0),
        "degree_gain": jnp.clip(jnp.exp(jax.random.uniform(streams_of[4], (FUNC, DEG), jnp.float32, math.log(0.5), math.log(2.0))), 0.5, 2.0),
        "legendre": draw_legendre(jax.random.fold_in(streams_of[7], 71), 0),
        "order_table": draw_order_table(jax.random.fold_in(streams_of[7], 71), 0),
    }


def angle_table(orders, first_lon, lon_count, period):
    longitude = first_lon + jnp.arange(lon_count, dtype=jnp.int32)
    phase_turns = (orders[:, None] * longitude[None, :]) % period
    phases = phase_turns.astype(jnp.float32) * (2.0 * math.pi / period)
    return jnp.stack([jnp.cos(phases), jnp.sin(phases)], 0).astype(jnp.bfloat16)


def synth_block(legendre_table, coefficients, orders, gains):
    slot_count, cycle_count, degree_count = legendre_table.shape
    funcs = gains.shape[0]
    half_deg = degree_count // 2
    scaled = (gains[:, None, None, :] * coefficients[None]).astype(jnp.bfloat16)
    scaled = lax.optimization_barrier(scaled).astype(jnp.float32)
    table_split = legendre_table.reshape(slot_count, cycle_count, half_deg, 2).astype(jnp.float32)
    scaled_split = scaled.reshape(funcs, slot_count, 2, half_deg, 2)
    legendre_parts = jnp.einsum('sjlt,fsclt->stfcj', table_split, scaled_split, precision=lax.Precision.HIGHEST)
    odd_order = (orders % 2 == 1)[:, None, None, None]
    first_part = legendre_parts[:, 0]
    second_part = legendre_parts[:, 1]
    even_part = jnp.where(odd_order, second_part, first_part)
    odd_part = jnp.where(odd_order, first_part, second_part)
    spectra = jnp.stack([even_part + odd_part, even_part - odd_part], -1)
    return spectra.reshape(slot_count, funcs, 2, 2 * cycle_count).astype(jnp.bfloat16)


def adjoint_block(legendre_table, returned, orders, gains):
    slot_count, cycle_count, degree_count = legendre_table.shape
    funcs = gains.shape[0]
    half_deg = degree_count // 2
    hemis = returned.reshape(slot_count, funcs, 2, cycle_count, 2).astype(jnp.float32)
    hemi_sum = (hemis[..., 0] + hemis[..., 1]).astype(jnp.bfloat16)
    hemi_diff = (hemis[..., 0] - hemis[..., 1]).astype(jnp.bfloat16)
    hemi_sum = lax.optimization_barrier(hemi_sum).astype(jnp.float32)
    hemi_diff = lax.optimization_barrier(hemi_diff).astype(jnp.float32)
    odd_order = (orders % 2 == 1)[:, None, None, None]
    combined = jnp.stack([jnp.where(odd_order, hemi_diff, hemi_sum), jnp.where(odd_order, hemi_sum, hemi_diff)], 1)
    table_split = legendre_table.reshape(slot_count, cycle_count, half_deg, 2).astype(jnp.float32)
    legendre_parts = jnp.einsum('sjlt,stfcj->sfclt', table_split, combined, precision=lax.Precision.HIGHEST)
    legendre_parts = legendre_parts.reshape(slot_count, funcs, 2, degree_count)
    return jnp.sum(gains[None, :, None, :] * legendre_parts, 1)


def reference(start, observed, coverage, class_weight, degree_gain, legendre, order_table):
    block_slots = 64
    block_count = NORD // block_slots
    scale = NLON ** -0.5
    fourier = lax.optimization_barrier(angle_table(order_table, 0, NLON, NLON)).astype(jnp.float32)
    legendre_blocks = legendre.reshape(block_count, block_slots, RH, DEG)
    order_blocks = order_table.reshape(block_count, block_slots)

    pair_index = jnp.arange(RH, dtype=jnp.int32)
    theta = (pair_index.astype(jnp.float32) + 0.5) * (math.pi / (2 * RH))
    area = jnp.repeat(jnp.sin(theta), 2)
    classes = jnp.arange(1, CLASSES + 1, dtype=jnp.int32)
    matched = coverage[..., None] == classes
    cell_weight = jnp.sum(jnp.where(matched, class_weight[:, None, None, :], 0.0), -1)
    weight = cell_weight * area[None, :, None]
    precondition = 1.0 / (jnp.arange(DEG, dtype=jnp.int32).astype(jnp.float32) + 1.0)

    def synth_one(pieces):
        return synth_block(pieces[0], pieces[1], pieces[2], degree_gain)

    def adjoint_one(pieces):
        return adjoint_block(pieces[0], pieces[1], pieces[2], degree_gain)

    def synthesize(coefficients):
        coef_blocks = coefficients.reshape(block_count, block_slots, 2, DEG)
        spectra = lax.map(synth_one, (legendre_blocks, coef_blocks, order_blocks))
        spectra = spectra.reshape(NORD, FUNC, 2, CYCLES).astype(jnp.float32)
        return scale * jnp.einsum('sfcr,csl->frl', spectra, fourier, precision=lax.Precision.HIGHEST)

    def analyze(weighted):
        rounded = lax.optimization_barrier(weighted.astype(jnp.bfloat16)).astype(jnp.float32)
        returned = scale * jnp.einsum('frl,csl->sfcr', rounded, fourier, precision=lax.Precision.HIGHEST)
        returned = returned.astype(jnp.bfloat16).reshape(block_count, block_slots, FUNC, 2, CYCLES)
        adjoint = lax.map(adjoint_one, (legendre_blocks, returned, order_blocks))
        return adjoint.reshape(NORD, 2, DEG)

    solution = start
    gradient = analyze(weight * (observed - synthesize(start)))
    scaled_grad = precondition * gradient
    energy = jnp.sum(gradient * scaled_grad)
    direction = scaled_grad
    for iteration in range(ITERS):
        synth_image = synthesize(direction)
        curvature = jnp.sum(weight * synth_image * synth_image)
        step_size = energy / curvature
        solution = solution + step_size * direction
        gradient = gradient - step_size * analyze(weight * synth_image)
        if iteration + 1 < ITERS:
            scaled_grad = precondition * gradient
            energy_next = jnp.sum(gradient * scaled_grad)
            direction = scaled_grad + (energy_next / energy) * direction
            energy = energy_next
    return solution, gradient
```

```python
import functools
import math

import jax
import jax.numpy as jnp
from jax import lax
from jax.experimental import pallas as pl
from jax.experimental.pallas import tpu as pltpu
from jax.sharding import PartitionSpec as P

ITERS = 2
MESH = pl.DeviceIdType.MESH


def exchange_kernel(blk_count, quarter_count, per_blk, send_ref, recv_ref, send_sem, recv_sem):
    total = blk_count * quarter_count
    blk = lax.axis_index("blk")
    quarter = lax.axis_index("quarter")
    me = blk * quarter_count + quarter
    barrier = pltpu.get_barrier_semaphore()

    def greet(i, carry):
        peer = lax.rem(me + i, total)
        pl.semaphore_signal(
            barrier,
            inc=1,
            device_id=(lax.div(peer, quarter_count), lax.rem(peer, quarter_count)),
            device_id_type=MESH,
        )
        return carry

    lax.fori_loop(1, total, greet, 0)
    recv_ref[me] = send_ref[blk if per_blk else me]
    pl.semaphore_wait(barrier, total - 1)

    def send(i, carry):
        peer = lax.rem(me + i, total)
        peer_blk = lax.div(peer, quarter_count)
        pltpu.make_async_remote_copy(
            src_ref=send_ref.at[peer_blk if per_blk else peer],
            dst_ref=recv_ref.at[me],
            send_sem=send_sem,
            recv_sem=recv_sem,
            device_id=(peer_blk, lax.rem(peer, quarter_count)),
            device_id_type=MESH,
        ).start()
        return carry

    lax.fori_loop(1, total, send, 0)
    landed = recv_ref.at[pl.ds(0, total - 1)]
    pltpu.make_async_copy(landed, landed, recv_sem).wait()
    pltpu.make_async_copy(landed, landed, send_sem).wait()


def exchange(messages, blk_count, quarter_count, per_blk):
    total = blk_count * quarter_count
    return pl.pallas_call(
        functools.partial(exchange_kernel, blk_count, quarter_count, per_blk),
        out_shape=jax.ShapeDtypeStruct((total,) + messages.shape[1:], messages.dtype),
        in_specs=[pl.BlockSpec(memory_space=pltpu.VMEM)],
        out_specs=pl.BlockSpec(memory_space=pltpu.VMEM),
        scratch_shapes=[pltpu.SemaphoreType.DMA(()), pltpu.SemaphoreType.DMA(())],
        compiler_params=pltpu.CompilerParams(
            collective_id=0 if per_blk else 1, has_side_effects=True, vmem_limit_bytes=32 << 20
        ),
        name="to_cycles" if per_blk else "to_orders",
    )(messages)


def half_turn_sine(phase, quarter_turn):
    z = phase.astype(jnp.float32) * (1.0 / quarter_turn)
    y = z * z
    acc = jnp.float32(-3.41817280e-06)
    for coef in (1.60217136e-04, -4.68162024e-03, 7.96925873e-02, -6.45964093e-01, 1.57079633):
        acc = acc * y + jnp.float32(coef)
    return acc * z


def cos_sin(steps, period):
    turn = jnp.bitwise_and(steps, period - 1)
    half = period // 2
    quarter = period // 4
    cosine = half_turn_sine(jnp.abs(turn - half) - quarter, quarter)
    shifted = jnp.bitwise_and(turn - quarter, period - 1)
    sine = half_turn_sine(jnp.abs(shifted - half) - quarter, quarter)
    return cosine, sine


def split_scalar(value, shape):
    hi = lax.reduce_precision(value, 8, 7)
    mid = lax.reduce_precision(value - hi, 8, 7)
    low = value - hi - mid
    lane = lax.broadcasted_iota(jnp.int32, shape, len(shape) - 1)
    zero = jnp.float32(0.0)
    picked = jnp.where(lane == 0, hi, jnp.where(lane == 1, mid, jnp.where(lane == 2, low, zero)))
    row = lax.broadcasted_iota(jnp.int32, shape, len(shape) - 2)
    return jnp.where(row == 0, picked, zero)


def body(start, observed, coverage, class_weight, degree_gain, legendre, order_table):
    blk_count = lax.axis_size("blk")
    quarter_count = lax.axis_size("quarter")
    blk_index = lax.axis_index("blk")
    quarter_index = lax.axis_index("quarter")
    total = blk_count * quarter_count
    slot_count, cycle_pairs, degree_count = legendre.shape
    order_count = order_table.shape[0]
    funcs, cycle_local, lon_local = observed.shape
    lon_total = lon_local * quarter_count
    half_lon = lon_local // 2
    rows = funcs * cycle_local
    lanes = 2 * slot_count
    pad_rows = -(rows + 1) % 16 + 1
    scale = lon_total ** (-0.5)
    bf16 = jnp.bfloat16
    first_slot = (blk_index * quarter_count + quarter_index) * slot_count
    my_orders = lax.dynamic_slice_in_dim(order_table, first_slot, slot_count)

    tile = min(128, half_lon)
    coarse = jnp.arange(half_lon // tile, dtype=jnp.int32) * tile
    fine = 2 * jnp.arange(tile, dtype=jnp.int32) + 1
    cos_a, sin_a = cos_sin(order_table[:, None] * (2 * coarse)[None, :], 2 * lon_total)
    cos_b, sin_b = cos_sin(order_table[:, None] * fine[None, :], 2 * lon_total)
    centre = 2 * lon_local * quarter_index + (lon_local - 1)
    cos_c, sin_c = cos_sin(order_table * centre, 2 * lon_total)
    cos_a, sin_a, cos_b, sin_b, cos_c, sin_c = lax.optimization_barrier(
        (cos_a, sin_a, cos_b, sin_b, cos_c, sin_c)
    )
    cos_table = jnp.concatenate(
        [cos_a[:, i : i + 1] * cos_b - sin_a[:, i : i + 1] * sin_b for i in range(coarse.shape[0])], 1
    ).astype(bf16)
    sin_table = jnp.concatenate(
        [sin_a[:, i : i + 1] * cos_b + cos_a[:, i : i + 1] * sin_b for i in range(coarse.shape[0])], 1
    ).astype(bf16)

    pair_index = blk_index * (cycle_local // 2) + jnp.arange(cycle_local // 2, dtype=jnp.int32)
    theta = (pair_index.astype(jnp.float32) + 0.5) * (math.pi / (2 * cycle_pairs))
    area = jnp.repeat(jnp.sin(theta), 2)
    classes = jnp.arange(1, class_weight.shape[1] + 1, dtype=jnp.int32)
    matched = coverage[..., None] == classes
    cell_weight = jnp.sum(jnp.where(matched, class_weight[:, None, None, :], 0.0), -1)
    weight = (cell_weight * area[None, :, None]).reshape(rows, lon_local)

    def fold(grid):
        return grid[:, half_lon:], jnp.flip(grid[:, :half_lon], 1)

    observed_plus, observed_minus = fold(observed.reshape(rows, lon_local))
    weight_plus, weight_minus = fold(weight)
    precondition = 1.0 / (jnp.arange(degree_count, dtype=jnp.int32).astype(jnp.float32) + 1.0)

    degrees = jnp.arange(degree_count, dtype=jnp.int32)
    even_mask = ((degrees[None, :] + my_orders[:, None]) % 2 == 0)[:, None, None, :]

    def to_grid(coefficients, partial):
        scaled = degree_gain[None, :, None, :] * coefficients[:, None]
        zeros = jnp.zeros_like(scaled)
        parity = jnp.stack(
            [jnp.where(even_mask, scaled, zeros), jnp.where(even_mask, zeros, scaled)], 1
        ).astype(bf16)
        parts = jnp.einsum("sjl,stfcl->tjfcs", legendre, parity, preferred_element_type=jnp.float32)
        spectra = jnp.stack([parts[0] + parts[1], parts[0] - parts[1]], 1)
        spectra = spectra.reshape(blk_count, cycle_local, funcs, lanes).transpose(0, 2, 1, 3)
        spectra = spectra.reshape(blk_count, rows, lanes)
        tail = jnp.broadcast_to(split_scalar(partial, (pad_rows, lanes)), (blk_count, pad_rows, lanes))
        messages = jnp.concatenate([spectra, tail], 1).astype(bf16)
        arrived = exchange(messages, blk_count, quarter_count, True).astype(jnp.float32)
        summed = jnp.sum(arrived[:, rows:])
        spectra = arrived[:, :rows].reshape(total, rows, 2, slot_count).transpose(2, 1, 0, 3)
        spectra = spectra.reshape(2, rows, order_count)
        real = (spectra[0] * cos_c + spectra[1] * sin_c).astype(bf16)
        imag = (spectra[1] * cos_c - spectra[0] * sin_c).astype(bf16)
        even = scale * jnp.dot(real, cos_table, preferred_element_type=jnp.float32)
        odd = scale * jnp.dot(imag, sin_table, preferred_element_type=jnp.float32)
        return even + odd, even - odd, summed

    def to_orders(plus, minus, partial):
        contract = (((1,), (1,)), ((), ()))
        even = lax.dot_general(
            (plus + minus).astype(bf16), cos_table, contract, preferred_element_type=jnp.float32
        )
        odd = lax.dot_general(
            (plus - minus).astype(bf16), sin_table, contract, preferred_element_type=jnp.float32
        )
        real = scale * (even * cos_c - odd * sin_c)
        imag = scale * (even * sin_c + odd * cos_c)
        shares = jnp.stack([real, imag], 1).reshape(rows, 2, total, slot_count).transpose(2, 0, 1, 3)
        shares = shares.reshape(total, rows, lanes)
        tail = jnp.broadcast_to(split_scalar(partial, (pad_rows, lanes)), (total, pad_rows, lanes))
        messages = jnp.concatenate([shares, tail], 1).astype(bf16)
        arrived = exchange(messages, blk_count, quarter_count, False).astype(jnp.float32)
        summed = jnp.sum(arrived[:, rows:])
        returned = jnp.sum(arrived[:, :rows].reshape(blk_count, quarter_count, rows, lanes), 1)
        returned = returned.reshape(blk_count, funcs, cycle_local // 2, 2, 2, slot_count)
        north, south = returned[:, :, :, 0], returned[:, :, :, 1]
        combined = jnp.stack([north + south, north - south], 0).astype(bf16)
        combined = combined.transpose(5, 0, 4, 2, 1, 3).reshape(slot_count, 2, 2, funcs, cycle_pairs)
        parts = jnp.einsum("sjl,sucfj->sucfl", legendre, combined, preferred_element_type=jnp.float32)
        picked = jnp.where(even_mask, parts[:, 0], parts[:, 1])
        return jnp.sum(degree_gain[None, None, :, :] * picked, 2), summed

    zero = jnp.float32(0.0)
    solution = start
    plus, minus, _ = to_grid(start, zero)
    gradient, _ = to_orders(
        weight_plus * (observed_plus - plus), weight_minus * (observed_minus - minus), zero
    )
    direction = energy = image = None
    for iteration in range(ITERS):
        scaled_grad = precondition * gradient
        plus, minus, energy_next = to_grid(scaled_grad, jnp.sum(gradient * scaled_grad))
        if iteration == 0:
            direction = scaled_grad
        else:
            ratio = energy_next / energy
            direction = scaled_grad + ratio * direction
            plus = plus + ratio * image[0]
            minus = minus + ratio * image[1]
        image = (plus, minus)
        energy = energy_next
        weighted_plus, weighted_minus = weight_plus * plus, weight_minus * minus
        partial = jnp.sum(weighted_plus * plus + weighted_minus * minus)
        change, curvature = to_orders(weighted_plus, weighted_minus, partial)
        step_size = energy / curvature
        solution = solution + step_size * direction
        gradient = gradient - step_size * change
    return (solution, gradient)


def solution(mesh):
    return jax.shard_map(
        body,
        mesh=mesh,
        in_specs=(
            P(("blk", "quarter"), None, None),
            P(None, "blk", "quarter"),
            P(None, "blk", "quarter"),
            P(),
            P(),
            P(("blk", "quarter"), None, None),
            P(),
        ),
        out_specs=(P(("blk", "quarter"), None, None), P(("blk", "quarter"), None, None)),
        check_vma=False,
    )
```

```python
import functools
import math

import jax
import jax.numpy as jnp
from jax import lax
from jax.experimental import pallas as pl
from jax.experimental.pallas import tpu as pltpu
from jax.sharding import PartitionSpec as P

ITERS = 2
MESH = pl.DeviceIdType.MESH


def exchange_kernel(blk_count, quarter_count, per_blk, send_ref, recv_ref, send_sem, recv_sem):
    total = blk_count * quarter_count
    blk = lax.axis_index("blk")
    quarter = lax.axis_index("quarter")
    me = blk * quarter_count + quarter
    barrier = pltpu.get_barrier_semaphore()

    def greet(i, carry):
        peer = lax.rem(me + i, total)
        pl.semaphore_signal(
            barrier,
            inc=1,
            device_id=(lax.div(peer, quarter_count), lax.rem(peer, quarter_count)),
            device_id_type=MESH,
        )
        return carry

    lax.fori_loop(1, total, greet, 0)
    recv_ref[me] = send_ref[blk if per_blk else me]
    pl.semaphore_wait(barrier, total - 1)

    def send(i, carry):
        peer = lax.rem(me + i, total)
        peer_blk = lax.div(peer, quarter_count)
        pltpu.make_async_remote_copy(
            src_ref=send_ref.at[peer_blk if per_blk else peer],
            dst_ref=recv_ref.at[me],
            send_sem=send_sem,
            recv_sem=recv_sem,
            device_id=(peer_blk, lax.rem(peer, quarter_count)),
            device_id_type=MESH,
        ).start()
        return carry

    lax.fori_loop(1, total, send, 0)
    landed = recv_ref.at[pl.ds(0, total - 1)]
    pltpu.make_async_copy(landed, landed, recv_sem).wait()
    pltpu.make_async_copy(landed, landed, send_sem).wait()


def exchange(messages, blk_count, quarter_count, per_blk):
    total = blk_count * quarter_count
    return pl.pallas_call(
        functools.partial(exchange_kernel, blk_count, quarter_count, per_blk),
        out_shape=jax.ShapeDtypeStruct((total,) + messages.shape[1:], messages.dtype),
        in_specs=[pl.BlockSpec(memory_space=pltpu.VMEM)],
        out_specs=pl.BlockSpec(memory_space=pltpu.VMEM),
        scratch_shapes=[pltpu.SemaphoreType.DMA(()), pltpu.SemaphoreType.DMA(())],
        compiler_params=pltpu.CompilerParams(
            collective_id=0 if per_blk else 1, has_side_effects=True, vmem_limit_bytes=32 << 20
        ),
        name="to_cycles" if per_blk else "to_orders",
    )(messages)


def scatter(me, blk_count, quarter_count, send_ref, per_blk, recv_ref, send_sem, recv_sem):
    total = blk_count * quarter_count

    def send(i, carry):
        peer = lax.rem(me + i, total)
        peer_blk = lax.div(peer, quarter_count)
        pltpu.make_async_remote_copy(
            src_ref=send_ref.at[peer_blk if per_blk else peer],
            dst_ref=recv_ref.at[me],
            send_sem=send_sem,
            recv_sem=recv_sem,
            device_id=(peer_blk, lax.rem(peer, quarter_count)),
            device_id_type=MESH,
        ).start()
        return carry

    lax.fori_loop(1, total, send, 0)


def grid_kernel(
    blk_count,
    quarter_count,
    scale,
    params_ref,
    send_ref,
    old_ref,
    weight_ref,
    cos_ref,
    sin_ref,
    table_ref,
    returned_ref,
    image_ref,
    sums_ref,
    arrived_ref,
    left_ref,
    shares_ref,
    landed_ref,
    send_sem,
    recv_sem,
):
    total = blk_count * quarter_count
    blk = lax.axis_index("blk")
    quarter = lax.axis_index("quarter")
    me = blk * quarter_count + quarter
    barrier = pltpu.get_barrier_semaphore()

    def greet(i, carry):
        peer = lax.rem(me + i, total)
        pl.semaphore_signal(
            barrier,
            inc=1,
            device_id=(lax.div(peer, quarter_count), lax.rem(peer, quarter_count)),
            device_id_type=MESH,
        )
        return carry

    lax.fori_loop(1, total, greet, 0)
    arrived_ref[me] = send_ref[blk]
    pl.semaphore_wait(barrier, total - 1)
    scatter(me, blk_count, quarter_count, send_ref, True, arrived_ref, send_sem.at[0], recv_sem.at[0])
    some = arrived_ref.at[pl.ds(0, total - 1)]
    pltpu.make_async_copy(some, some, recv_sem.at[0]).wait()

    arrived = arrived_ref[...].astype(jnp.float32)
    rows = arrived.shape[1] // 2
    lanes = arrived.shape[2]
    lane = lax.broadcasted_iota(jnp.int32, (1, 1, lanes), 2)
    sign = jnp.where(lane < lanes // 2, jnp.float32(1.0), jnp.float32(-1.0))
    values = arrived[:, :rows]
    turned = values * cos_ref[...] + pltpu.roll(values, lanes // 2, 2) * sin_ref[...]
    left = jnp.concatenate([turned, turned * sign], 1).astype(jnp.bfloat16)
    for d in range(total):
        left_ref[:, d * lanes : (d + 1) * lanes] = left[d]
    tail = jnp.sum(arrived[:, rows:], 0)
    energy = jnp.sum(jnp.sum(tail, 1, keepdims=True), 0, keepdims=True)

    field = scale * jnp.dot(left_ref[...], table_ref[...], preferred_element_type=jnp.float32)
    params = params_ref[...]
    ratio = params[1:2, 0:1] + params[2:3, 0:1] * energy / params[3:4, 0:1]
    image = params[0:1, 0:1] * field + ratio * old_ref[...]
    image_ref[...] = image
    weighted = weight_ref[...] * image
    partial = jnp.sum(weighted * image, 0, keepdims=True)
    partial = sum(partial[:, i : i + lanes] for i in range(0, partial.shape[1], lanes))
    high = partial.astype(jnp.bfloat16).astype(jnp.float32)
    middle = (partial - high).astype(jnp.bfloat16).astype(jnp.float32)
    low = partial - high - middle
    row = lax.broadcasted_iota(jnp.int32, (rows, lanes), 0)
    tail = jnp.where(row == 0, high, jnp.where(row == 1, middle, jnp.where(row == 2, low, 0.0)))
    plus, minus = weighted[:rows], weighted[rows:]
    folded = jnp.concatenate([plus + minus, plus - minus], 0).astype(jnp.bfloat16)
    back = lax.dot_general(
        folded, table_ref[...], (((1,), (1,)), ((), ())), preferred_element_type=jnp.float32
    )
    cos_lanes = lax.broadcasted_iota(jnp.int32, (rows, lanes), 1) < lanes // 2
    for d in range(total):
        part = back[:, d * lanes : (d + 1) * lanes]
        picked = scale * jnp.where(cos_lanes, part[:rows], part[rows:])
        share = picked * cos_ref[d] - pltpu.roll(picked, lanes // 2, 1) * sin_ref[d]
        shares_ref[d] = jnp.concatenate([share, tail], 0).astype(jnp.bfloat16)

    landed_ref[me] = shares_ref[me]
    scatter(me, blk_count, quarter_count, shares_ref, False, landed_ref, send_sem.at[1], recv_sem.at[1])
    some = landed_ref.at[pl.ds(0, total - 1)]
    pltpu.make_async_copy(some, some, recv_sem.at[1]).wait()
    landed = landed_ref[...].astype(jnp.float32)
    for b in range(blk_count):
        returned_ref[b] = sum(landed[b * quarter_count + q, :rows] for q in range(quarter_count))
    tail = jnp.sum(landed[:, rows:], 0)
    curvature = jnp.sum(jnp.sum(tail, 1, keepdims=True), 0, keepdims=True)
    sums_ref[...] = jnp.where(row == 0, energy, curvature)
    pltpu.make_async_copy(some, some, send_sem.at[0]).wait()
    pltpu.make_async_copy(some, some, send_sem.at[1]).wait()


def grid_stage(params, messages, old, weight, cos_rot, sin_rot, table, blk_count, quarter_count, scale):
    total = blk_count * quarter_count
    block_rows, lanes = messages.shape[1:]
    rows = block_rows // 2
    block = (total, block_rows, lanes)
    return pl.pallas_call(
        functools.partial(grid_kernel, blk_count, quarter_count, scale),
        out_shape=(
            jax.ShapeDtypeStruct((blk_count, rows, lanes), jnp.float32),
            jax.ShapeDtypeStruct(old.shape, jnp.float32),
            jax.ShapeDtypeStruct((rows, lanes), jnp.float32),
        ),
        in_specs=[pl.BlockSpec(memory_space=pltpu.VMEM)] * 7,
        out_specs=(pl.BlockSpec(memory_space=pltpu.VMEM),) * 3,
        scratch_shapes=[
            pltpu.VMEM(block, jnp.bfloat16),
            pltpu.VMEM((block_rows, total * lanes), jnp.bfloat16),
            pltpu.VMEM(block, jnp.bfloat16),
            pltpu.VMEM(block, jnp.bfloat16),
            pltpu.SemaphoreType.DMA((2,)),
            pltpu.SemaphoreType.DMA((2,)),
        ],
        compiler_params=pltpu.CompilerParams(
            collective_id=2, has_side_effects=True, vmem_limit_bytes=24 << 20
        ),
        name="grid_stage",
    )(params, messages, old, weight, cos_rot, sin_rot, table)


def half_turn_sine(phase, quarter_turn):
    z = phase.astype(jnp.float32) * (1.0 / quarter_turn)
    y = z * z
    acc = jnp.float32(-3.41817280e-06)
    for coef in (1.60217136e-04, -4.68162024e-03, 7.96925873e-02, -6.45964093e-01, 1.57079633):
        acc = acc * y + jnp.float32(coef)
    return acc * z


def cos_sin(steps, period):
    turn = jnp.bitwise_and(steps, period - 1)
    half = period // 2
    quarter = period // 4
    cosine = half_turn_sine(jnp.abs(turn - half) - quarter, quarter)
    shifted = jnp.bitwise_and(turn - quarter, period - 1)
    sine = half_turn_sine(jnp.abs(shifted - half) - quarter, quarter)
    return cosine, sine


def split_scalar(value, shape):
    hi = lax.reduce_precision(value, 8, 7)
    mid = lax.reduce_precision(value - hi, 8, 7)
    low = value - hi - mid
    lane = lax.broadcasted_iota(jnp.int32, shape, len(shape) - 1)
    zero = jnp.float32(0.0)
    picked = jnp.where(lane == 0, hi, jnp.where(lane == 1, mid, jnp.where(lane == 2, low, zero)))
    row = lax.broadcasted_iota(jnp.int32, shape, len(shape) - 2)
    return jnp.where(row == 0, picked, zero)


def body(start, observed, coverage, class_weight, degree_gain, legendre, order_table):
    blk_count = lax.axis_size("blk")
    quarter_count = lax.axis_size("quarter")
    blk_index = lax.axis_index("blk")
    quarter_index = lax.axis_index("quarter")
    total = blk_count * quarter_count
    slot_count, cycle_pairs, degree_count = legendre.shape
    order_count = order_table.shape[0]
    funcs, cycle_local, lon_local = observed.shape
    lon_total = lon_local * quarter_count
    half_lon = lon_local // 2
    rows = funcs * cycle_local
    lanes = 2 * slot_count
    pad_rows = -(rows + 1) % 16 + 1
    scale = lon_total ** (-0.5)
    bf16 = jnp.bfloat16
    first_slot = (blk_index * quarter_count + quarter_index) * slot_count
    my_orders = lax.dynamic_slice_in_dim(order_table, first_slot, slot_count)

    tile = min(128, half_lon)
    coarse = jnp.arange(half_lon // tile, dtype=jnp.int32) * tile
    fine = 2 * jnp.arange(tile, dtype=jnp.int32) + 1
    cos_a, sin_a = cos_sin(order_table[:, None] * (2 * coarse)[None, :], 2 * lon_total)
    cos_b, sin_b = cos_sin(order_table[:, None] * fine[None, :], 2 * lon_total)
    centre = 2 * lon_local * quarter_index + (lon_local - 1)
    cos_c, sin_c = cos_sin(order_table * centre, 2 * lon_total)
    cos_a, sin_a, cos_b, sin_b, cos_c, sin_c = lax.optimization_barrier(
        (cos_a, sin_a, cos_b, sin_b, cos_c, sin_c)
    )
    cos_table = jnp.concatenate(
        [cos_a[:, i : i + 1] * cos_b - sin_a[:, i : i + 1] * sin_b for i in range(coarse.shape[0])], 1
    ).astype(bf16)
    sin_table = jnp.concatenate(
        [sin_a[:, i : i + 1] * cos_b + cos_a[:, i : i + 1] * sin_b for i in range(coarse.shape[0])], 1
    ).astype(bf16)
    fused = lanes == 128 and 2 * rows == 16 and pad_rows == rows
    if fused:
        table = jnp.concatenate(
            [
                cos_table.reshape(total, slot_count, half_lon),
                sin_table.reshape(total, slot_count, half_lon),
            ],
            1,
        ).reshape(total * lanes, half_lon)
        cos_c = cos_c.reshape(total, 1, slot_count)
        sin_c = sin_c.reshape(total, 1, slot_count)
        cos_rot = jnp.concatenate([cos_c, cos_c], 2)
        sin_rot = jnp.concatenate([sin_c, -sin_c], 2)

    pair_index = blk_index * (cycle_local // 2) + jnp.arange(cycle_local // 2, dtype=jnp.int32)
    theta = (pair_index.astype(jnp.float32) + 0.5) * (math.pi / (2 * cycle_pairs))
    area = jnp.repeat(jnp.sin(theta), 2)
    classes = jnp.arange(1, class_weight.shape[1] + 1, dtype=jnp.int32)
    matched = coverage[..., None] == classes
    cell_weight = jnp.sum(jnp.where(matched, class_weight[:, None, None, :], 0.0), -1)
    weight = (cell_weight * area[None, :, None]).reshape(rows, lon_local)

    def fold(grid):
        return grid[:, half_lon:], jnp.flip(grid[:, :half_lon], 1)

    observed_plus, observed_minus = fold(observed.reshape(rows, lon_local))
    weight_plus, weight_minus = fold(weight)
    precondition = 1.0 / (jnp.arange(degree_count, dtype=jnp.int32).astype(jnp.float32) + 1.0)

    degrees = jnp.arange(degree_count, dtype=jnp.int32)
    even_mask = ((degrees[None, :] + my_orders[:, None]) % 2 == 0)[:, None, None, :]

    def to_messages(coefficients, partial):
        scaled = degree_gain[None, :, None, :] * coefficients[:, None]
        zeros = jnp.zeros_like(scaled)
        parity = jnp.stack(
            [jnp.where(even_mask, scaled, zeros), jnp.where(even_mask, zeros, scaled)], 1
        ).astype(bf16)
        parts = jnp.einsum("sjl,stfcl->tjfcs", legendre, parity, preferred_element_type=jnp.float32)
        spectra = jnp.stack([parts[0] + parts[1], parts[0] - parts[1]], 1)
        spectra = spectra.reshape(blk_count, cycle_local, funcs, lanes).transpose(0, 2, 1, 3)
        spectra = spectra.reshape(blk_count, rows, lanes)
        tail = jnp.broadcast_to(split_scalar(partial, (pad_rows, lanes)), (blk_count, pad_rows, lanes))
        return jnp.concatenate([spectra, tail], 1).astype(bf16)

    def to_grid(coefficients, partial):
        messages = to_messages(coefficients, partial)
        arrived = exchange(messages, blk_count, quarter_count, True).astype(jnp.float32)
        summed = jnp.sum(arrived[:, rows:])
        spectra = arrived[:, :rows].reshape(total, rows, 2, slot_count).transpose(2, 1, 0, 3)
        spectra = spectra.reshape(2, rows, order_count)
        real = (spectra[0] * cos_c + spectra[1] * sin_c).astype(bf16)
        imag = (spectra[1] * cos_c - spectra[0] * sin_c).astype(bf16)
        even = scale * jnp.dot(real, cos_table, preferred_element_type=jnp.float32)
        odd = scale * jnp.dot(imag, sin_table, preferred_element_type=jnp.float32)
        return even + odd, even - odd, summed

    def to_orders(plus, minus, partial):
        contract = (((1,), (1,)), ((), ()))
        even = lax.dot_general(
            (plus + minus).astype(bf16), cos_table, contract, preferred_element_type=jnp.float32
        )
        odd = lax.dot_general(
            (plus - minus).astype(bf16), sin_table, contract, preferred_element_type=jnp.float32
        )
        real = scale * (even * cos_c - odd * sin_c)
        imag = scale * (even * sin_c + odd * cos_c)
        shares = jnp.stack([real, imag], 1).reshape(rows, 2, total, slot_count).transpose(2, 0, 1, 3)
        shares = shares.reshape(total, rows, lanes)
        tail = jnp.broadcast_to(split_scalar(partial, (pad_rows, lanes)), (total, pad_rows, lanes))
        messages = jnp.concatenate([shares, tail], 1).astype(bf16)
        arrived = exchange(messages, blk_count, quarter_count, False).astype(jnp.float32)
        summed = jnp.sum(arrived[:, rows:])
        returned = jnp.sum(arrived[:, :rows].reshape(blk_count, quarter_count, rows, lanes), 1)
        return to_coefficients(returned), summed

    def to_coefficients(returned):
        returned = returned.reshape(blk_count, funcs, cycle_local // 2, 2, 2, slot_count)
        north, south = returned[:, :, :, 0], returned[:, :, :, 1]
        combined = jnp.stack([north + south, north - south], 0).astype(bf16)
        combined = combined.transpose(5, 0, 4, 2, 1, 3).reshape(slot_count, 2, 2, funcs, cycle_pairs)
        parts = jnp.einsum("sjl,sucfj->sucfl", legendre, combined, preferred_element_type=jnp.float32)
        picked = jnp.where(even_mask, parts[:, 0], parts[:, 1])
        return jnp.sum(degree_gain[None, None, :, :] * picked, 2)

    zero = jnp.float32(0.0)
    one = jnp.float32(1.0)
    solution = start
    if fused:
        stacked_weight = jnp.concatenate([weight_plus, weight_minus], 0)
        image = jnp.concatenate([observed_plus, observed_minus], 0)

        def stage(factors, coefficients, partial, old):
            params = jnp.broadcast_to(jnp.stack(factors + [zero] * 4)[:, None], (8, lanes))
            returned, image, sums = grid_stage(
                params, to_messages(coefficients, partial), old, stacked_weight,
                cos_rot, sin_rot, table, blk_count, quarter_count, scale,
            )
            return to_coefficients(returned), image, sums[0, 0], sums[1, 0]

        gradient, _, _, _ = stage([-one, one, zero, one], start, zero, image)
        direction = energy = None
        for iteration in range(ITERS):
            scaled_grad = precondition * gradient
            factors = [one, zero, zero, one] if iteration == 0 else [one, zero, one, energy]
            change, image, energy_next, curvature = stage(
                factors, scaled_grad, jnp.sum(gradient * scaled_grad), image
            )
            if iteration == 0:
                direction = scaled_grad
            else:
                direction = scaled_grad + energy_next / energy * direction
            energy = energy_next
            step_size = energy / curvature
            solution = solution + step_size * direction
            gradient = gradient - step_size * change
        return (solution, gradient)
    plus, minus, _ = to_grid(start, zero)
    gradient, _ = to_orders(
        weight_plus * (observed_plus - plus), weight_minus * (observed_minus - minus), zero
    )
    direction = energy = image = None
    for iteration in range(ITERS):
        scaled_grad = precondition * gradient
        plus, minus, energy_next = to_grid(scaled_grad, jnp.sum(gradient * scaled_grad))
        if iteration == 0:
            direction = scaled_grad
        else:
            ratio = energy_next / energy
            direction = scaled_grad + ratio * direction
            plus = plus + ratio * image[0]
            minus = minus + ratio * image[1]
        image = (plus, minus)
        energy = energy_next
        weighted_plus, weighted_minus = weight_plus * plus, weight_minus * minus
        partial = jnp.sum(weighted_plus * plus + weighted_minus * minus)
        change, curvature = to_orders(weighted_plus, weighted_minus, partial)
        step_size = energy / curvature
        solution = solution + step_size * direction
        gradient = gradient - step_size * change
    return (solution, gradient)


def solution(mesh):
    return jax.shard_map(
        body,
        mesh=mesh,
        in_specs=(
            P(("blk", "quarter"), None, None),
            P(None, "blk", "quarter"),
            P(None, "blk", "quarter"),
            P(),
            P(),
            P(("blk", "quarter"), None, None),
            P(),
        ),
        out_specs=(P(("blk", "quarter"), None, None), P(("blk", "quarter"), None, None)),
        check_vma=False,
    )
```

```python
import functools
import math

import jax
import jax.numpy as jnp
from jax import lax
from jax.experimental import pallas as pl
from jax.experimental.pallas import tpu as pltpu
from jax.sharding import PartitionSpec as P

ITERS = 2
MESH = pl.DeviceIdType.MESH


def exchange_kernel(blk_count, quarter_count, per_blk, send_ref, recv_ref, send_sem, recv_sem):
    total = blk_count * quarter_count
    blk = lax.axis_index("blk")
    quarter = lax.axis_index("quarter")
    me = blk * quarter_count + quarter
    barrier = pltpu.get_barrier_semaphore()

    def greet(i, carry):
        peer = lax.rem(me + i, total)
        pl.semaphore_signal(
            barrier,
            inc=1,
            device_id=(lax.div(peer, quarter_count), lax.rem(peer, quarter_count)),
            device_id_type=MESH,
        )
        return carry

    lax.fori_loop(1, total, greet, 0)
    recv_ref[me] = send_ref[blk if per_blk else me]
    pl.semaphore_wait(barrier, total - 1)

    def send(i, carry):
        peer = lax.rem(me + i, total)
        peer_blk = lax.div(peer, quarter_count)
        pltpu.make_async_remote_copy(
            src_ref=send_ref.at[peer_blk if per_blk else peer],
            dst_ref=recv_ref.at[me],
            send_sem=send_sem,
            recv_sem=recv_sem,
            device_id=(peer_blk, lax.rem(peer, quarter_count)),
            device_id_type=MESH,
        ).start()
        return carry

    lax.fori_loop(1, total, send, 0)
    landed = recv_ref.at[pl.ds(0, total - 1)]
    pltpu.make_async_copy(landed, landed, recv_sem).wait()
    pltpu.make_async_copy(landed, landed, send_sem).wait()


def exchange(messages, blk_count, quarter_count, per_blk):
    total = blk_count * quarter_count
    return pl.pallas_call(
        functools.partial(exchange_kernel, blk_count, quarter_count, per_blk),
        out_shape=jax.ShapeDtypeStruct((total,) + messages.shape[1:], messages.dtype),
        in_specs=[pl.BlockSpec(memory_space=pltpu.VMEM)],
        out_specs=pl.BlockSpec(memory_space=pltpu.VMEM),
        scratch_shapes=[pltpu.SemaphoreType.DMA(()), pltpu.SemaphoreType.DMA(())],
        compiler_params=pltpu.CompilerParams(
            collective_id=0 if per_blk else 1, has_side_effects=True, vmem_limit_bytes=32 << 20
        ),
        name="to_cycles" if per_blk else "to_orders",
    )(messages)


def scatter(me, blk_count, quarter_count, send_ref, per_blk, recv_ref, send_sem, recv_sem):
    total = blk_count * quarter_count

    def send(i, carry):
        peer = lax.rem(me + i, total)
        peer_blk = lax.div(peer, quarter_count)
        pltpu.make_async_remote_copy(
            src_ref=send_ref.at[peer_blk if per_blk else peer],
            dst_ref=recv_ref.at[me],
            send_sem=send_sem,
            recv_sem=recv_sem,
            device_id=(peer_blk, lax.rem(peer, quarter_count)),
            device_id_type=MESH,
        ).start()
        return carry

    lax.fori_loop(1, total, send, 0)


def grid_kernel(
    blk_count,
    quarter_count,
    scale,
    params_ref,
    send_ref,
    old_ref,
    weight_ref,
    cos_ref,
    sin_ref,
    table_ref,
    returned_ref,
    image_ref,
    sums_ref,
    arrived_ref,
    left_ref,
    shares_ref,
    landed_ref,
    send_sem,
    recv_sem,
):
    total = blk_count * quarter_count
    blk = lax.axis_index("blk")
    quarter = lax.axis_index("quarter")
    me = blk * quarter_count + quarter
    barrier = pltpu.get_barrier_semaphore()

    def greet(i, carry):
        peer = lax.rem(me + i, total)
        pl.semaphore_signal(
            barrier,
            inc=1,
            device_id=(lax.div(peer, quarter_count), lax.rem(peer, quarter_count)),
            device_id_type=MESH,
        )
        return carry

    lax.fori_loop(1, total, greet, 0)
    arrived_ref[me] = send_ref[blk]
    pl.semaphore_wait(barrier, total - 1)
    scatter(me, blk_count, quarter_count, send_ref, True, arrived_ref, send_sem.at[0], recv_sem.at[0])
    some = arrived_ref.at[pl.ds(0, total - 1)]
    pltpu.make_async_copy(some, some, recv_sem.at[0]).wait()

    arrived = arrived_ref[...].astype(jnp.float32)
    rows = arrived.shape[1] // 2
    lanes = arrived.shape[2]
    lane = lax.broadcasted_iota(jnp.int32, (1, 1, lanes), 2)
    sign = jnp.where(lane < lanes // 2, jnp.float32(1.0), jnp.float32(-1.0))
    values = arrived[:, :rows]
    turned = values * cos_ref[...] + pltpu.roll(values, lanes // 2, 2) * sin_ref[...]
    left = jnp.concatenate([turned, turned * sign], 1).astype(jnp.bfloat16)
    for d in range(total):
        left_ref[:, d * lanes : (d + 1) * lanes] = left[d]
    tail = jnp.sum(arrived[:, rows:], 0)
    energy = jnp.sum(jnp.sum(tail, 1, keepdims=True), 0, keepdims=True)

    field = scale * jnp.dot(left_ref[...], table_ref[...], preferred_element_type=jnp.float32)
    params = params_ref[...]
    ratio = params[1:2, 0:1] + params[2:3, 0:1] * energy / params[3:4, 0:1]
    image = params[0:1, 0:1] * field + ratio * old_ref[...]
    image_ref[...] = image
    weighted = weight_ref[...] * image
    partial = jnp.sum(weighted * image, 0, keepdims=True)
    partial = sum(partial[:, i : i + lanes] for i in range(0, partial.shape[1], lanes))
    high = partial.astype(jnp.bfloat16).astype(jnp.float32)
    middle = (partial - high).astype(jnp.bfloat16).astype(jnp.float32)
    low = partial - high - middle
    row = lax.broadcasted_iota(jnp.int32, (rows, lanes), 0)
    tail = jnp.where(row == 0, high, jnp.where(row == 1, middle, jnp.where(row == 2, low, 0.0)))
    plus, minus = weighted[:rows], weighted[rows:]
    folded = jnp.concatenate([plus + minus, plus - minus], 0).astype(jnp.bfloat16)
    back = lax.dot_general(
        folded, table_ref[...], (((1,), (1,)), ((), ())), preferred_element_type=jnp.float32
    )
    cos_lanes = lax.broadcasted_iota(jnp.int32, (rows, lanes), 1) < lanes // 2
    for d in range(total):
        part = back[:, d * lanes : (d + 1) * lanes]
        picked = scale * jnp.where(cos_lanes, part[:rows], part[rows:])
        share = picked * cos_ref[d] - pltpu.roll(picked, lanes // 2, 1) * sin_ref[d]
        shares_ref[d] = jnp.concatenate([share, tail], 0).astype(jnp.bfloat16)

    landed_ref[me] = shares_ref[me]
    scatter(me, blk_count, quarter_count, shares_ref, False, landed_ref, send_sem.at[1], recv_sem.at[1])
    some = landed_ref.at[pl.ds(0, total - 1)]
    pltpu.make_async_copy(some, some, recv_sem.at[1]).wait()
    landed = landed_ref[...].astype(jnp.float32)
    for b in range(blk_count):
        returned_ref[b] = sum(landed[b * quarter_count + q, :rows] for q in range(quarter_count))
    tail = jnp.sum(landed[:, rows:], 0)
    curvature = jnp.sum(jnp.sum(tail, 1, keepdims=True), 0, keepdims=True)
    sums_ref[...] = jnp.where(row == 0, energy, curvature)
    pltpu.make_async_copy(some, some, send_sem.at[0]).wait()
    pltpu.make_async_copy(some, some, send_sem.at[1]).wait()


def grid_stage(params, messages, old, weight, cos_rot, sin_rot, table, blk_count, quarter_count, scale):
    total = blk_count * quarter_count
    block_rows, lanes = messages.shape[1:]
    rows = block_rows // 2
    block = (total, block_rows, lanes)
    return pl.pallas_call(
        functools.partial(grid_kernel, blk_count, quarter_count, scale),
        out_shape=(
            jax.ShapeDtypeStruct((blk_count, rows, lanes), jnp.float32),
            jax.ShapeDtypeStruct(old.shape, jnp.float32),
            jax.ShapeDtypeStruct((rows, lanes), jnp.float32),
        ),
        in_specs=[pl.BlockSpec(memory_space=pltpu.VMEM)] * 7,
        out_specs=(pl.BlockSpec(memory_space=pltpu.VMEM),) * 3,
        scratch_shapes=[
            pltpu.VMEM(block, jnp.bfloat16),
            pltpu.VMEM((block_rows, total * lanes), jnp.bfloat16),
            pltpu.VMEM(block, jnp.bfloat16),
            pltpu.VMEM(block, jnp.bfloat16),
            pltpu.SemaphoreType.DMA((2,)),
            pltpu.SemaphoreType.DMA((2,)),
        ],
        compiler_params=pltpu.CompilerParams(
            collective_id=2, has_side_effects=True, vmem_limit_bytes=24 << 20
        ),
        name="grid_stage",
    )(params, messages, old, weight, cos_rot, sin_rot, table)


def synth_kernel(
    blk_count, values_ref, factor_ref, gain_ref, sign_ref, legendre_ref, message_ref, right_ref, rows_ref
):
    lanes, degree_count = values_ref.shape
    slot_count = lanes // 2
    funcs = gain_ref.shape[0]
    values = values_ref[...]
    scaled = factor_ref[...] * values
    lane_sign = 1 - 2 * (lax.broadcasted_iota(jnp.int32, (1, degree_count), 1) % 2)
    sign = sign_ref[...] * lane_sign.astype(jnp.float32)
    partial = jnp.sum(values * scaled, 0, keepdims=True)
    partial = sum(partial[:, i : i + lanes] for i in range(0, degree_count, lanes))
    high = partial.astype(jnp.bfloat16).astype(jnp.float32)
    middle = (partial - high).astype(jnp.bfloat16).astype(jnp.float32)
    low = partial - high - middle
    row = lax.broadcasted_iota(jnp.int32, (8, lanes), 0)
    tail = jnp.where(row == 0, high, jnp.where(row == 1, middle, jnp.where(row == 2, low, 0.0)))
    slot = lax.broadcasted_iota(jnp.int32, (slot_count, 2 * lanes), 0)
    lane = lax.broadcasted_iota(jnp.int32, (slot_count, 2 * lanes), 1)
    own = slot == lane % slot_count
    for f in range(funcs):
        north = gain_ref[f : f + 1, :] * scaled
        right_ref[:lanes] = north.astype(jnp.bfloat16)
        right_ref[lanes:] = (north * sign).astype(jnp.bfloat16)
        parts = lax.dot_general(
            legendre_ref[...], right_ref[...], (((1,), (1,)), ((), ())),
            preferred_element_type=jnp.float32,
        )
        for j in range(blk_count):
            part = parts[j * slot_count : (j + 1) * slot_count]
            kept = jnp.sum(jnp.where(own, part, 0.0), 0, keepdims=True)
            rows_ref[j, 2 * f : 2 * f + 1, :] = kept[:, :lanes]
            rows_ref[j, 2 * f + 1 : 2 * f + 2, :] = kept[:, lanes:]
    for j in range(blk_count):
        message_ref[j] = jnp.concatenate([rows_ref[j], tail], 0).astype(jnp.bfloat16)


def synth_stage(values, factor, gains, sign, legendre_rows, blk_count):
    lanes, degree_count = values.shape
    rows = 2 * gains.shape[0]
    return pl.pallas_call(
        functools.partial(synth_kernel, blk_count),
        out_shape=jax.ShapeDtypeStruct((blk_count, 2 * rows, lanes), jnp.bfloat16),
        in_specs=[pl.BlockSpec(memory_space=pltpu.VMEM)] * 5,
        out_specs=pl.BlockSpec(memory_space=pltpu.VMEM),
        scratch_shapes=[
            pltpu.VMEM((2 * lanes, degree_count), jnp.bfloat16),
            pltpu.VMEM((blk_count, rows, lanes), jnp.float32),
        ],
        compiler_params=pltpu.CompilerParams(vmem_limit_bytes=24 << 20),
        name="synth_stage",
    )(values, factor, gains, sign, legendre_rows)


def adjoint_kernel(blk_count, returned_ref, gain_ref, sign_ref, legendre_ref, change_ref, left_ref):
    lanes, degree_count = change_ref.shape
    slot_count = lanes // 2
    funcs = gain_ref.shape[0]
    slot = lax.broadcasted_iota(jnp.int32, (slot_count, lanes), 0)
    lane = lax.broadcasted_iota(jnp.int32, (slot_count, lanes), 1)
    own = slot == lane % slot_count
    first = lax.broadcasted_iota(jnp.int32, (1, lanes), 1) < slot_count
    for a in range(blk_count // 2):
        near, far = returned_ref[2 * a], returned_ref[2 * a + 1]
        near_turned, far_turned = pltpu.roll(near, slot_count, 1), pltpu.roll(far, slot_count, 1)
        parts = (jnp.where(first, near, far_turned), jnp.where(first, near_turned, far))
        for c in range(2):
            for f in range(funcs):
                north = parts[c][2 * f : 2 * f + 1]
                south = parts[c][2 * f + 1 : 2 * f + 2]
                for u, hemis in enumerate((north + south, north - south)):
                    at = ((c * funcs + f) * 2 + u) * slot_count
                    left_ref[at : at + slot_count, a * lanes : (a + 1) * lanes] = jnp.where(
                        own, hemis, 0.0
                    ).astype(jnp.bfloat16)
    width = 256
    even_lane = lax.broadcasted_iota(jnp.int32, (slot_count, width), 1) % 2 == 0
    even_order = sign_ref[:slot_count, :] > 0.0
    even = even_lane == even_order
    for at in range(0, degree_count, width):
        parts = jnp.dot(
            left_ref[...], legendre_ref[:, at : at + width], preferred_element_type=jnp.float32
        )
        for c in range(2):
            total = None
            for f in range(funcs):
                base = (c * funcs + f) * 2 * slot_count
                picked = jnp.where(
                    even, parts[base : base + slot_count],
                    parts[base + slot_count : base + 2 * slot_count],
                )
                term = gain_ref[f : f + 1, at : at + width] * picked
                total = term if f == 0 else total + term
            change_ref[c * slot_count : (c + 1) * slot_count, at : at + width] = total


def adjoint_stage(returned, gains, sign, legendre_rows):
    blk_count, rows, lanes = returned.shape
    degree_count = legendre_rows.shape[1]
    return pl.pallas_call(
        functools.partial(adjoint_kernel, blk_count),
        out_shape=jax.ShapeDtypeStruct((lanes, degree_count), jnp.float32),
        in_specs=[pl.BlockSpec(memory_space=pltpu.VMEM)] * 4,
        out_specs=pl.BlockSpec(memory_space=pltpu.VMEM),
        scratch_shapes=[pltpu.VMEM((rows * lanes, legendre_rows.shape[0]), jnp.bfloat16)],
        compiler_params=pltpu.CompilerParams(vmem_limit_bytes=24 << 20),
        name="adjoint_stage",
    )(returned, gains, sign, legendre_rows)


def half_turn_sine(phase, quarter_turn):
    z = phase.astype(jnp.float32) * (1.0 / quarter_turn)
    y = z * z
    acc = jnp.float32(-3.41817280e-06)
    for coef in (1.60217136e-04, -4.68162024e-03, 7.96925873e-02, -6.45964093e-01, 1.57079633):
        acc = acc * y + jnp.float32(coef)
    return acc * z


def cos_sin(steps, period):
    turn = jnp.bitwise_and(steps, period - 1)
    half = period // 2
    quarter = period // 4
    cosine = half_turn_sine(jnp.abs(turn - half) - quarter, quarter)
    shifted = jnp.bitwise_and(turn - quarter, period - 1)
    sine = half_turn_sine(jnp.abs(shifted - half) - quarter, quarter)
    return cosine, sine


def split_scalar(value, shape):
    hi = lax.reduce_precision(value, 8, 7)
    mid = lax.reduce_precision(value - hi, 8, 7)
    low = value - hi - mid
    lane = lax.broadcasted_iota(jnp.int32, shape, len(shape) - 1)
    zero = jnp.float32(0.0)
    picked = jnp.where(lane == 0, hi, jnp.where(lane == 1, mid, jnp.where(lane == 2, low, zero)))
    row = lax.broadcasted_iota(jnp.int32, shape, len(shape) - 2)
    return jnp.where(row == 0, picked, zero)


def body(start, observed, coverage, class_weight, degree_gain, legendre, order_table):
    blk_count = lax.axis_size("blk")
    quarter_count = lax.axis_size("quarter")
    blk_index = lax.axis_index("blk")
    quarter_index = lax.axis_index("quarter")
    total = blk_count * quarter_count
    slot_count, cycle_pairs, degree_count = legendre.shape
    order_count = order_table.shape[0]
    funcs, cycle_local, lon_local = observed.shape
    lon_total = lon_local * quarter_count
    half_lon = lon_local // 2
    rows = funcs * cycle_local
    lanes = 2 * slot_count
    pad_rows = -(rows + 1) % 16 + 1
    scale = lon_total ** (-0.5)
    bf16 = jnp.bfloat16
    first_slot = (blk_index * quarter_count + quarter_index) * slot_count
    my_orders = lax.dynamic_slice_in_dim(order_table, first_slot, slot_count)

    tile = min(128, half_lon)
    coarse = jnp.arange(half_lon // tile, dtype=jnp.int32) * tile
    fine = 2 * jnp.arange(tile, dtype=jnp.int32) + 1
    cos_a, sin_a = cos_sin(order_table[:, None] * (2 * coarse)[None, :], 2 * lon_total)
    cos_b, sin_b = cos_sin(order_table[:, None] * fine[None, :], 2 * lon_total)
    centre = 2 * lon_local * quarter_index + (lon_local - 1)
    cos_c, sin_c = cos_sin(order_table * centre, 2 * lon_total)
    cos_a, sin_a, cos_b, sin_b, cos_c, sin_c = lax.optimization_barrier(
        (cos_a, sin_a, cos_b, sin_b, cos_c, sin_c)
    )
    cos_table = jnp.concatenate(
        [cos_a[:, i : i + 1] * cos_b - sin_a[:, i : i + 1] * sin_b for i in range(coarse.shape[0])], 1
    ).astype(bf16)
    sin_table = jnp.concatenate(
        [sin_a[:, i : i + 1] * cos_b + cos_a[:, i : i + 1] * sin_b for i in range(coarse.shape[0])], 1
    ).astype(bf16)
    fused = lanes == 128 and rows == 8 and cycle_local == 2 and cycle_pairs == blk_count
    if fused:
        table = jnp.concatenate(
            [
                cos_table.reshape(total, slot_count, half_lon),
                sin_table.reshape(total, slot_count, half_lon),
            ],
            1,
        ).reshape(total * lanes, half_lon)
        cos_c = cos_c.reshape(total, 1, slot_count)
        sin_c = sin_c.reshape(total, 1, slot_count)
        cos_rot = jnp.concatenate([cos_c, cos_c], 2)
        sin_rot = jnp.concatenate([sin_c, -sin_c], 2)

    pair_index = blk_index * (cycle_local // 2) + jnp.arange(cycle_local // 2, dtype=jnp.int32)
    theta = (pair_index.astype(jnp.float32) + 0.5) * (math.pi / (2 * cycle_pairs))
    area = jnp.repeat(jnp.sin(theta), 2)
    classes = jnp.arange(1, class_weight.shape[1] + 1, dtype=jnp.int32)
    matched = coverage[..., None] == classes
    cell_weight = jnp.sum(jnp.where(matched, class_weight[:, None, None, :], 0.0), -1)
    weight = (cell_weight * area[None, :, None]).reshape(rows, lon_local)

    def fold(grid):
        return grid[:, half_lon:], jnp.flip(grid[:, :half_lon], 1)

    observed_plus, observed_minus = fold(observed.reshape(rows, lon_local))
    weight_plus, weight_minus = fold(weight)
    precondition = 1.0 / (jnp.arange(degree_count, dtype=jnp.int32).astype(jnp.float32) + 1.0)

    degrees = jnp.arange(degree_count, dtype=jnp.int32)
    even_mask = ((degrees[None, :] + my_orders[:, None]) % 2 == 0)[:, None, None, :]

    def to_messages(coefficients, partial):
        scaled = degree_gain[None, :, None, :] * coefficients[:, None]
        zeros = jnp.zeros_like(scaled)
        parity = jnp.stack(
            [jnp.where(even_mask, scaled, zeros), jnp.where(even_mask, zeros, scaled)], 1
        ).astype(bf16)
        parts = jnp.einsum("sjl,stfcl->tjfcs", legendre, parity, preferred_element_type=jnp.float32)
        spectra = jnp.stack([parts[0] + parts[1], parts[0] - parts[1]], 1)
        spectra = spectra.reshape(blk_count, cycle_local, funcs, lanes).transpose(0, 2, 1, 3)
        spectra = spectra.reshape(blk_count, rows, lanes)
        tail = jnp.broadcast_to(split_scalar(partial, (pad_rows, lanes)), (blk_count, pad_rows, lanes))
        return jnp.concatenate([spectra, tail], 1).astype(bf16)

    def to_grid(coefficients, partial):
        messages = to_messages(coefficients, partial)
        arrived = exchange(messages, blk_count, quarter_count, True).astype(jnp.float32)
        summed = jnp.sum(arrived[:, rows:])
        spectra = arrived[:, :rows].reshape(total, rows, 2, slot_count).transpose(2, 1, 0, 3)
        spectra = spectra.reshape(2, rows, order_count)
        real = (spectra[0] * cos_c + spectra[1] * sin_c).astype(bf16)
        imag = (spectra[1] * cos_c - spectra[0] * sin_c).astype(bf16)
        even = scale * jnp.dot(real, cos_table, preferred_element_type=jnp.float32)
        odd = scale * jnp.dot(imag, sin_table, preferred_element_type=jnp.float32)
        return even + odd, even - odd, summed

    def to_orders(plus, minus, partial):
        contract = (((1,), (1,)), ((), ()))
        even = lax.dot_general(
            (plus + minus).astype(bf16), cos_table, contract, preferred_element_type=jnp.float32
        )
        odd = lax.dot_general(
            (plus - minus).astype(bf16), sin_table, contract, preferred_element_type=jnp.float32
        )
        real = scale * (even * cos_c - odd * sin_c)
        imag = scale * (even * sin_c + odd * cos_c)
        shares = jnp.stack([real, imag], 1).reshape(rows, 2, total, slot_count).transpose(2, 0, 1, 3)
        shares = shares.reshape(total, rows, lanes)
        tail = jnp.broadcast_to(split_scalar(partial, (pad_rows, lanes)), (total, pad_rows, lanes))
        messages = jnp.concatenate([shares, tail], 1).astype(bf16)
        arrived = exchange(messages, blk_count, quarter_count, False).astype(jnp.float32)
        summed = jnp.sum(arrived[:, rows:])
        returned = jnp.sum(arrived[:, :rows].reshape(blk_count, quarter_count, rows, lanes), 1)
        return to_coefficients(returned), summed

    def to_coefficients(returned):
        returned = returned.reshape(blk_count, funcs, cycle_local // 2, 2, 2, slot_count)
        north, south = returned[:, :, :, 0], returned[:, :, :, 1]
        combined = jnp.stack([north + south, north - south], 0).astype(bf16)
        combined = combined.transpose(5, 0, 4, 2, 1, 3).reshape(slot_count, 2, 2, funcs, cycle_pairs)
        parts = jnp.einsum("sjl,sucfj->sucfl", legendre, combined, preferred_element_type=jnp.float32)
        picked = jnp.where(even_mask, parts[:, 0], parts[:, 1])
        return jnp.sum(degree_gain[None, None, :, :] * picked, 2)

    zero = jnp.float32(0.0)
    one = jnp.float32(1.0)
    solution = start
    if fused:
        stacked_weight = jnp.concatenate([weight_plus, weight_minus], 0)
        image = jnp.concatenate([observed_plus, observed_minus], 0)
        legendre_rows = legendre.transpose(1, 0, 2).reshape(cycle_pairs * slot_count, degree_count)
        order_sign = (1 - 2 * (my_orders % 2)).astype(jnp.float32)
        order_sign = jnp.concatenate([order_sign, order_sign])[:, None]
        factor = precondition[None, :]

        def stage(factors, coefficients, multiplier, old):
            params = jnp.broadcast_to(jnp.stack(factors + [zero] * 4)[:, None], (8, lanes))
            messages = synth_stage(
                coefficients, multiplier, degree_gain, order_sign, legendre_rows, blk_count
            )
            returned, image, sums = grid_stage(
                params, messages, old, stacked_weight,
                cos_rot, sin_rot, table, blk_count, quarter_count, scale,
            )
            change = adjoint_stage(returned, degree_gain, order_sign, legendre_rows)
            return change, image, sums[0, 0], sums[1, 0]

        solution = start.transpose(1, 0, 2).reshape(lanes, degree_count)
        gradient, _, _, _ = stage([-one, one, zero, one], solution, jnp.ones_like(factor), image)
        direction = energy = None
        for iteration in range(ITERS):
            scaled_grad = factor * gradient
            factors = [one, zero, zero, one] if iteration == 0 else [one, zero, one, energy]
            change, image, energy_next, curvature = stage(factors, gradient, factor, image)
            if iteration == 0:
                direction = scaled_grad
            else:
                direction = scaled_grad + energy_next / energy * direction
            energy = energy_next
            step_size = energy / curvature
            solution = solution + step_size * direction
            gradient = gradient - step_size * change
        return tuple(
            out.reshape(2, slot_count, degree_count).transpose(1, 0, 2) for out in (solution, gradient)
        )
    plus, minus, _ = to_grid(start, zero)
    gradient, _ = to_orders(
        weight_plus * (observed_plus - plus), weight_minus * (observed_minus - minus), zero
    )
    direction = energy = image = None
    for iteration in range(ITERS):
        scaled_grad = precondition * gradient
        plus, minus, energy_next = to_grid(scaled_grad, jnp.sum(gradient * scaled_grad))
        if iteration == 0:
            direction = scaled_grad
        else:
            ratio = energy_next / energy
            direction = scaled_grad + ratio * direction
            plus = plus + ratio * image[0]
            minus = minus + ratio * image[1]
        image = (plus, minus)
        energy = energy_next
        weighted_plus, weighted_minus = weight_plus * plus, weight_minus * minus
        partial = jnp.sum(weighted_plus * plus + weighted_minus * minus)
        change, curvature = to_orders(weighted_plus, weighted_minus, partial)
        step_size = energy / curvature
        solution = solution + step_size * direction
        gradient = gradient - step_size * change
    return (solution, gradient)


def solution(mesh):
    return jax.shard_map(
        body,
        mesh=mesh,
        in_specs=(
            P(("blk", "quarter"), None, None),
            P(None, "blk", "quarter"),
            P(None, "blk", "quarter"),
            P(),
            P(),
            P(("blk", "quarter"), None, None),
            P(),
        ),
        out_specs=(P(("blk", "quarter"), None, None), P(("blk", "quarter"), None, None)),
        check_vma=False,
    )
```

```python
import functools
import math

import jax
import jax.numpy as jnp
from jax import lax
from jax.experimental import pallas as pl
from jax.experimental.pallas import tpu as pltpu
from jax.sharding import PartitionSpec as P

ITERS = 2
MESH = pl.DeviceIdType.MESH


def exchange_kernel(blk_count, quarter_count, per_blk, send_ref, recv_ref, send_sem, recv_sem):
    total = blk_count * quarter_count
    blk = lax.axis_index("blk")
    quarter = lax.axis_index("quarter")
    me = blk * quarter_count + quarter
    barrier = pltpu.get_barrier_semaphore()

    def greet(i, carry):
        peer = lax.rem(me + i, total)
        pl.semaphore_signal(
            barrier,
            inc=1,
            device_id=(lax.div(peer, quarter_count), lax.rem(peer, quarter_count)),
            device_id_type=MESH,
        )
        return carry

    lax.fori_loop(1, total, greet, 0)
    recv_ref[me] = send_ref[blk if per_blk else me]
    pl.semaphore_wait(barrier, total - 1)

    def send(i, carry):
        peer = lax.rem(me + i, total)
        peer_blk = lax.div(peer, quarter_count)
        pltpu.make_async_remote_copy(
            src_ref=send_ref.at[peer_blk if per_blk else peer],
            dst_ref=recv_ref.at[me],
            send_sem=send_sem,
            recv_sem=recv_sem,
            device_id=(peer_blk, lax.rem(peer, quarter_count)),
            device_id_type=MESH,
        ).start()
        return carry

    lax.fori_loop(1, total, send, 0)
    landed = recv_ref.at[pl.ds(0, total - 1)]
    pltpu.make_async_copy(landed, landed, recv_sem).wait()
    pltpu.make_async_copy(landed, landed, send_sem).wait()


def exchange(messages, blk_count, quarter_count, per_blk):
    total = blk_count * quarter_count
    return pl.pallas_call(
        functools.partial(exchange_kernel, blk_count, quarter_count, per_blk),
        out_shape=jax.ShapeDtypeStruct((total,) + messages.shape[1:], messages.dtype),
        in_specs=[pl.BlockSpec(memory_space=pltpu.VMEM)],
        out_specs=pl.BlockSpec(memory_space=pltpu.VMEM),
        scratch_shapes=[pltpu.SemaphoreType.DMA(()), pltpu.SemaphoreType.DMA(())],
        compiler_params=pltpu.CompilerParams(
            collective_id=0 if per_blk else 1, has_side_effects=True, vmem_limit_bytes=32 << 20
        ),
        name="to_cycles" if per_blk else "to_orders",
    )(messages)


def peers(blk_count, quarter_count, act):
    blk = lax.axis_index("blk")
    quarter = lax.axis_index("quarter")
    quarters = [lax.rem(quarter + i, quarter_count) for i in range(quarter_count)]
    for other in quarters[1:]:
        act(blk, other)

    def visit(i, carry):
        other_blk = lax.rem(blk + i, blk_count)
        for other in quarters:
            act(other_blk, other)
        return carry

    lax.fori_loop(1, blk_count, visit, 0)


def scatter(me, blk_count, quarter_count, send_ref, per_blk, recv_ref, send_sem, recv_sem):
    def send(peer_blk, peer_quarter):
        pltpu.make_async_remote_copy(
            src_ref=send_ref.at[peer_blk if per_blk else peer_blk * quarter_count + peer_quarter],
            dst_ref=recv_ref.at[me],
            send_sem=send_sem,
            recv_sem=recv_sem,
            device_id=(peer_blk, peer_quarter),
            device_id_type=MESH,
        ).start()

    peers(blk_count, quarter_count, send)


def grid_kernel(
    blk_count,
    quarter_count,
    scale,
    params_ref,
    send_ref,
    old_ref,
    weight_ref,
    cos_ref,
    sin_ref,
    table_ref,
    returned_ref,
    image_ref,
    sums_ref,
    arrived_ref,
    left_ref,
    shares_ref,
    landed_ref,
    send_sem,
    recv_sem,
):
    total = blk_count * quarter_count
    blk = lax.axis_index("blk")
    quarter = lax.axis_index("quarter")
    me = blk * quarter_count + quarter
    barrier = pltpu.get_barrier_semaphore()

    def greet(peer_blk, peer_quarter):
        pl.semaphore_signal(
            barrier, inc=1, device_id=(peer_blk, peer_quarter), device_id_type=MESH
        )

    peers(blk_count, quarter_count, greet)
    arrived_ref[me] = send_ref[blk]
    pl.semaphore_wait(barrier, total - 1)
    scatter(me, blk_count, quarter_count, send_ref, True, arrived_ref, send_sem.at[0], recv_sem.at[0])
    some = arrived_ref.at[pl.ds(0, total - 1)]
    pltpu.make_async_copy(some, some, recv_sem.at[0]).wait()

    arrived = arrived_ref[...].astype(jnp.float32)
    rows = arrived.shape[1] // 2
    lanes = arrived.shape[2]
    lane = lax.broadcasted_iota(jnp.int32, (1, 1, lanes), 2)
    sign = jnp.where(lane < lanes // 2, jnp.float32(1.0), jnp.float32(-1.0))
    values = arrived[:, :rows]
    turned = values * cos_ref[...] + pltpu.roll(values, lanes // 2, 2) * sin_ref[...]
    left = jnp.concatenate([turned, turned * sign], 1).astype(jnp.bfloat16)
    for d in range(total):
        left_ref[:, d * lanes : (d + 1) * lanes] = left[d]
    tail = jnp.sum(arrived[:, rows:], 0)
    energy = jnp.sum(jnp.sum(tail, 1, keepdims=True), 0, keepdims=True)

    field = scale * jnp.dot(left_ref[...], table_ref[...], preferred_element_type=jnp.float32)
    params = params_ref[...]
    ratio = params[1:2, 0:1] + params[2:3, 0:1] * energy / params[3:4, 0:1]
    image = params[0:1, 0:1] * field + ratio * old_ref[...]
    image_ref[...] = image
    weighted = weight_ref[...] * image
    partial = jnp.sum(weighted * image, 0, keepdims=True)
    partial = sum(partial[:, i : i + lanes] for i in range(0, partial.shape[1], lanes))
    high = partial.astype(jnp.bfloat16).astype(jnp.float32)
    middle = (partial - high).astype(jnp.bfloat16).astype(jnp.float32)
    low = partial - high - middle
    row = lax.broadcasted_iota(jnp.int32, (rows, lanes), 0)
    tail = jnp.where(row == 0, high, jnp.where(row == 1, middle, jnp.where(row == 2, low, 0.0)))
    plus, minus = weighted[:rows], weighted[rows:]
    folded = jnp.concatenate([plus + minus, plus - minus], 0).astype(jnp.bfloat16)
    back = lax.dot_general(
        folded, table_ref[...], (((1,), (1,)), ((), ())), preferred_element_type=jnp.float32
    )
    cos_lanes = lax.broadcasted_iota(jnp.int32, (rows, lanes), 1) < lanes // 2
    for d in range(total):
        part = back[:, d * lanes : (d + 1) * lanes]
        picked = scale * jnp.where(cos_lanes, part[:rows], part[rows:])
        share = picked * cos_ref[d] - pltpu.roll(picked, lanes // 2, 1) * sin_ref[d]
        shares_ref[d] = jnp.concatenate([share, tail], 0).astype(jnp.bfloat16)

    landed_ref[me] = shares_ref[me]
    scatter(me, blk_count, quarter_count, shares_ref, False, landed_ref, send_sem.at[1], recv_sem.at[1])
    some = landed_ref.at[pl.ds(0, total - 1)]
    pltpu.make_async_copy(some, some, recv_sem.at[1]).wait()
    landed = landed_ref[...].astype(jnp.float32)
    for b in range(blk_count):
        returned_ref[b] = sum(landed[b * quarter_count + q, :rows] for q in range(quarter_count))
    tail = jnp.sum(landed[:, rows:], 0)
    curvature = jnp.sum(jnp.sum(tail, 1, keepdims=True), 0, keepdims=True)
    sums_ref[...] = jnp.where(row == 0, energy, curvature)
    pltpu.make_async_copy(some, some, send_sem.at[0]).wait()
    pltpu.make_async_copy(some, some, send_sem.at[1]).wait()


def grid_stage(params, messages, old, weight, cos_rot, sin_rot, table, blk_count, quarter_count, scale):
    total = blk_count * quarter_count
    block_rows, lanes = messages.shape[1:]
    rows = block_rows // 2
    block = (total, block_rows, lanes)
    return pl.pallas_call(
        functools.partial(grid_kernel, blk_count, quarter_count, scale),
        out_shape=(
            jax.ShapeDtypeStruct((blk_count, rows, lanes), jnp.float32),
            jax.ShapeDtypeStruct(old.shape, jnp.float32),
            jax.ShapeDtypeStruct((rows, lanes), jnp.float32),
        ),
        in_specs=[pl.BlockSpec(memory_space=pltpu.VMEM)] * 7,
        out_specs=(pl.BlockSpec(memory_space=pltpu.VMEM),) * 3,
        scratch_shapes=[
            pltpu.VMEM(block, jnp.bfloat16),
            pltpu.VMEM((block_rows, total * lanes), jnp.bfloat16),
            pltpu.VMEM(block, jnp.bfloat16),
            pltpu.VMEM(block, jnp.bfloat16),
            pltpu.SemaphoreType.DMA((2,)),
            pltpu.SemaphoreType.DMA((2,)),
        ],
        compiler_params=pltpu.CompilerParams(
            collective_id=2, has_side_effects=True, vmem_limit_bytes=14 << 20
        ),
        name="grid_stage",
    )(params, messages, old, weight, cos_rot, sin_rot, table)


def synth_kernel(
    blk_count, values_ref, factor_ref, gain_ref, sign_ref, legendre_ref, message_ref, right_ref, rows_ref
):
    lanes, degree_count = values_ref.shape
    slot_count = lanes // 2
    funcs = gain_ref.shape[0]
    values = values_ref[...]
    scaled = factor_ref[...] * values
    lane_sign = 1 - 2 * (lax.broadcasted_iota(jnp.int32, (1, degree_count), 1) % 2)
    sign = sign_ref[...] * lane_sign.astype(jnp.float32)
    partial = jnp.sum(values * scaled, 0, keepdims=True)
    partial = sum(partial[:, i : i + lanes] for i in range(0, degree_count, lanes))
    high = partial.astype(jnp.bfloat16).astype(jnp.float32)
    middle = (partial - high).astype(jnp.bfloat16).astype(jnp.float32)
    low = partial - high - middle
    row = lax.broadcasted_iota(jnp.int32, (8, lanes), 0)
    tail = jnp.where(row == 0, high, jnp.where(row == 1, middle, jnp.where(row == 2, low, 0.0)))
    slot = lax.broadcasted_iota(jnp.int32, (slot_count, 2 * lanes), 0)
    lane = lax.broadcasted_iota(jnp.int32, (slot_count, 2 * lanes), 1)
    own = slot == lane % slot_count
    for f in range(funcs):
        north = gain_ref[f : f + 1, :] * scaled
        right_ref[:lanes] = north.astype(jnp.bfloat16)
        right_ref[lanes:] = (north * sign).astype(jnp.bfloat16)
        parts = lax.dot_general(
            legendre_ref[...], right_ref[...], (((1,), (1,)), ((), ())),
            preferred_element_type=jnp.float32,
        )
        for j in range(blk_count):
            part = parts[j * slot_count : (j + 1) * slot_count]
            kept = jnp.sum(jnp.where(own, part, 0.0), 0, keepdims=True)
            rows_ref[j, 2 * f : 2 * f + 1, :] = kept[:, :lanes]
            rows_ref[j, 2 * f + 1 : 2 * f + 2, :] = kept[:, lanes:]
    for j in range(blk_count):
        message_ref[j] = jnp.concatenate([rows_ref[j], tail], 0).astype(jnp.bfloat16)


def synth_stage(values, factor, gains, sign, legendre_rows, blk_count):
    lanes, degree_count = values.shape
    rows = 2 * gains.shape[0]
    return pl.pallas_call(
        functools.partial(synth_kernel, blk_count),
        out_shape=jax.ShapeDtypeStruct((blk_count, 2 * rows, lanes), jnp.bfloat16),
        in_specs=[pl.BlockSpec(memory_space=pltpu.VMEM)] * 5,
        out_specs=pl.BlockSpec(memory_space=pltpu.VMEM),
        scratch_shapes=[
            pltpu.VMEM((2 * lanes, degree_count), jnp.bfloat16),
            pltpu.VMEM((blk_count, rows, lanes), jnp.float32),
        ],
        compiler_params=pltpu.CompilerParams(vmem_limit_bytes=14 << 20),
        name="synth_stage",
    )(values, factor, gains, sign, legendre_rows)


def adjoint_kernel(blk_count, returned_ref, gain_ref, sign_ref, legendre_ref, change_ref, left_ref):
    lanes, degree_count = change_ref.shape
    slot_count = lanes // 2
    funcs = gain_ref.shape[0]
    slot = lax.broadcasted_iota(jnp.int32, (slot_count, lanes), 0)
    lane = lax.broadcasted_iota(jnp.int32, (slot_count, lanes), 1)
    own = slot == lane % slot_count
    first = lax.broadcasted_iota(jnp.int32, (1, lanes), 1) < slot_count
    for a in range(blk_count // 2):
        near, far = returned_ref[2 * a], returned_ref[2 * a + 1]
        near_turned, far_turned = pltpu.roll(near, slot_count, 1), pltpu.roll(far, slot_count, 1)
        parts = (jnp.where(first, near, far_turned), jnp.where(first, near_turned, far))
        for c in range(2):
            for f in range(funcs):
                north = parts[c][2 * f : 2 * f + 1]
                south = parts[c][2 * f + 1 : 2 * f + 2]
                for u, hemis in enumerate((north + south, north - south)):
                    at = ((c * funcs + f) * 2 + u) * slot_count
                    left_ref[at : at + slot_count, a * lanes : (a + 1) * lanes] = jnp.where(
                        own, hemis, 0.0
                    ).astype(jnp.bfloat16)
    width = 256
    even_lane = lax.broadcasted_iota(jnp.int32, (slot_count, width), 1) % 2 == 0
    even_order = sign_ref[:slot_count, :] > 0.0
    even = even_lane == even_order
    for at in range(0, degree_count, width):
        parts = jnp.dot(
            left_ref[...], legendre_ref[:, at : at + width], preferred_element_type=jnp.float32
        )
        for c in range(2):
            total = None
            for f in range(funcs):
                base = (c * funcs + f) * 2 * slot_count
                picked = jnp.where(
                    even, parts[base : base + slot_count],
                    parts[base + slot_count : base + 2 * slot_count],
                )
                term = gain_ref[f : f + 1, at : at + width] * picked
                total = term if f == 0 else total + term
            change_ref[c * slot_count : (c + 1) * slot_count, at : at + width] = total


def adjoint_stage(returned, gains, sign, legendre_rows):
    blk_count, rows, lanes = returned.shape
    degree_count = legendre_rows.shape[1]
    return pl.pallas_call(
        functools.partial(adjoint_kernel, blk_count),
        out_shape=jax.ShapeDtypeStruct((lanes, degree_count), jnp.float32),
        in_specs=[pl.BlockSpec(memory_space=pltpu.VMEM)] * 4,
        out_specs=pl.BlockSpec(memory_space=pltpu.VMEM),
        scratch_shapes=[pltpu.VMEM((rows * lanes, legendre_rows.shape[0]), jnp.bfloat16)],
        compiler_params=pltpu.CompilerParams(vmem_limit_bytes=14 << 20),
        name="adjoint_stage",
    )(returned, gains, sign, legendre_rows)


def half_turn_sine(phase, quarter_turn):
    z = phase.astype(jnp.float32) * (1.0 / quarter_turn)
    y = z * z
    acc = jnp.float32(-3.41817280e-06)
    for coef in (1.60217136e-04, -4.68162024e-03, 7.96925873e-02, -6.45964093e-01, 1.57079633):
        acc = acc * y + jnp.float32(coef)
    return acc * z


def table_kernel(total, order_ref, table_ref):
    rows, half_lon = table_ref.shape
    slot_count = rows // total // 2
    period = 4 * half_lon * lax.axis_size("quarter")
    lane = lax.broadcasted_iota(jnp.int32, (slot_count, 128), 1)

    def fill(d, carry):
        orders = order_ref[pl.ds(pl.multiple_of(d * slot_count, slot_count), slot_count), :]
        cos_b, sin_b = cos_sin(orders * (2 * lane + 1), period)
        cos_a, sin_a = cos_sin(orders * (256 * lane), period)
        at = pl.multiple_of(d * 2 * slot_count, 2 * slot_count)
        for i in range(half_lon // 128):
            cos_i, sin_i = cos_a[:, i : i + 1], sin_a[:, i : i + 1]
            lon = slice(i * 128, (i + 1) * 128)
            cosine = cos_i * cos_b - sin_i * sin_b
            sine = sin_i * cos_b + cos_i * sin_b
            table_ref[pl.ds(at, 2 * slot_count), lon] = jnp.concatenate([cosine, sine], 0).astype(
                jnp.bfloat16
            )
        return carry

    lax.fori_loop(0, total, fill, 0)


def table_stage(orders, total, half_lon):
    return pl.pallas_call(
        functools.partial(table_kernel, total),
        out_shape=jax.ShapeDtypeStruct((2 * orders.shape[0], half_lon), jnp.bfloat16),
        in_specs=[pl.BlockSpec(memory_space=pltpu.VMEM)],
        out_specs=pl.BlockSpec(memory_space=pltpu.VMEM),
        compiler_params=pltpu.CompilerParams(vmem_limit_bytes=14 << 20),
        name="table_stage",
    )(orders)


def cos_sin(steps, period):
    turn = jnp.bitwise_and(steps, period - 1)
    half = period // 2
    quarter = period // 4
    cosine = half_turn_sine(jnp.abs(turn - half) - quarter, quarter)
    shifted = jnp.bitwise_and(turn - quarter, period - 1)
    sine = half_turn_sine(jnp.abs(shifted - half) - quarter, quarter)
    return cosine, sine


def split_scalar(value, shape):
    hi = lax.reduce_precision(value, 8, 7)
    mid = lax.reduce_precision(value - hi, 8, 7)
    low = value - hi - mid
    lane = lax.broadcasted_iota(jnp.int32, shape, len(shape) - 1)
    zero = jnp.float32(0.0)
    picked = jnp.where(lane == 0, hi, jnp.where(lane == 1, mid, jnp.where(lane == 2, low, zero)))
    row = lax.broadcasted_iota(jnp.int32, shape, len(shape) - 2)
    return jnp.where(row == 0, picked, zero)


def body(start, observed, coverage, class_weight, degree_gain, legendre, order_table):
    blk_count = lax.axis_size("blk")
    quarter_count = lax.axis_size("quarter")
    blk_index = lax.axis_index("blk")
    quarter_index = lax.axis_index("quarter")
    total = blk_count * quarter_count
    slot_count, cycle_pairs, degree_count = legendre.shape
    order_count = order_table.shape[0]
    funcs, cycle_local, lon_local = observed.shape
    lon_total = lon_local * quarter_count
    half_lon = lon_local // 2
    rows = funcs * cycle_local
    lanes = 2 * slot_count
    pad_rows = -(rows + 1) % 16 + 1
    scale = lon_total ** (-0.5)
    bf16 = jnp.bfloat16
    first_slot = (blk_index * quarter_count + quarter_index) * slot_count
    my_orders = lax.dynamic_slice_in_dim(order_table, first_slot, slot_count)

    fused = lanes == 128 and rows == 8 and cycle_local == 2 and cycle_pairs == blk_count and half_lon % 128 == 0
    centre = 2 * lon_local * quarter_index + (lon_local - 1)
    cos_c, sin_c = cos_sin(order_table * centre, 2 * lon_total)
    if fused:
        table = table_stage(order_table[:, None], total, half_lon)
        cos_c = cos_c.reshape(total, 1, slot_count)
        sin_c = sin_c.reshape(total, 1, slot_count)
        cos_rot = jnp.concatenate([cos_c, cos_c], 2)
        sin_rot = jnp.concatenate([sin_c, -sin_c], 2)
    else:
        tile = min(128, half_lon)
        coarse = jnp.arange(half_lon // tile, dtype=jnp.int32) * tile
        fine = 2 * jnp.arange(tile, dtype=jnp.int32) + 1
        cos_a, sin_a = cos_sin(order_table[:, None] * (2 * coarse)[None, :], 2 * lon_total)
        cos_b, sin_b = cos_sin(order_table[:, None] * fine[None, :], 2 * lon_total)
        cos_a, sin_a, cos_b, sin_b, cos_c, sin_c = lax.optimization_barrier(
            (cos_a, sin_a, cos_b, sin_b, cos_c, sin_c)
        )
        cos_table = jnp.concatenate(
            [cos_a[:, i : i + 1] * cos_b - sin_a[:, i : i + 1] * sin_b for i in range(coarse.shape[0])], 1
        ).astype(bf16)
        sin_table = jnp.concatenate(
            [sin_a[:, i : i + 1] * cos_b + cos_a[:, i : i + 1] * sin_b for i in range(coarse.shape[0])], 1
        ).astype(bf16)

    pair_index = blk_index * (cycle_local // 2) + jnp.arange(cycle_local // 2, dtype=jnp.int32)
    theta = (pair_index.astype(jnp.float32) + 0.5) * (math.pi / (2 * cycle_pairs))
    area = jnp.repeat(jnp.sin(theta), 2)
    classes = jnp.arange(1, class_weight.shape[1] + 1, dtype=jnp.int32)
    matched = coverage[..., None] == classes
    cell_weight = jnp.sum(jnp.where(matched, class_weight[:, None, None, :], 0.0), -1)
    weight = (cell_weight * area[None, :, None]).reshape(rows, lon_local)

    def fold(grid):
        return grid[:, half_lon:], jnp.flip(grid[:, :half_lon], 1)

    observed_plus, observed_minus = fold(observed.reshape(rows, lon_local))
    weight_plus, weight_minus = fold(weight)
    precondition = 1.0 / (jnp.arange(degree_count, dtype=jnp.int32).astype(jnp.float32) + 1.0)

    degrees = jnp.arange(degree_count, dtype=jnp.int32)
    even_mask = ((degrees[None, :] + my_orders[:, None]) % 2 == 0)[:, None, None, :]

    def to_messages(coefficients, partial):
        scaled = degree_gain[None, :, None, :] * coefficients[:, None]
        zeros = jnp.zeros_like(scaled)
        parity = jnp.stack(
            [jnp.where(even_mask, scaled, zeros), jnp.where(even_mask, zeros, scaled)], 1
        ).astype(bf16)
        parts = jnp.einsum("sjl,stfcl->tjfcs", legendre, parity, preferred_element_type=jnp.float32)
        spectra = jnp.stack([parts[0] + parts[1], parts[0] - parts[1]], 1)
        spectra = spectra.reshape(blk_count, cycle_local, funcs, lanes).transpose(0, 2, 1, 3)
        spectra = spectra.reshape(blk_count, rows, lanes)
        tail = jnp.broadcast_to(split_scalar(partial, (pad_rows, lanes)), (blk_count, pad_rows, lanes))
        return jnp.concatenate([spectra, tail], 1).astype(bf16)

    def to_grid(coefficients, partial):
        messages = to_messages(coefficients, partial)
        arrived = exchange(messages, blk_count, quarter_count, True).astype(jnp.float32)
        summed = jnp.sum(arrived[:, rows:])
        spectra = arrived[:, :rows].reshape(total, rows, 2, slot_count).transpose(2, 1, 0, 3)
        spectra = spectra.reshape(2, rows, order_count)
        real = (spectra[0] * cos_c + spectra[1] * sin_c).astype(bf16)
        imag = (spectra[1] * cos_c - spectra[0] * sin_c).astype(bf16)
        even = scale * jnp.dot(real, cos_table, preferred_element_type=jnp.float32)
        odd = scale * jnp.dot(imag, sin_table, preferred_element_type=jnp.float32)
        return even + odd, even - odd, summed

    def to_orders(plus, minus, partial):
        contract = (((1,), (1,)), ((), ()))
        even = lax.dot_general(
            (plus + minus).astype(bf16), cos_table, contract, preferred_element_type=jnp.float32
        )
        odd = lax.dot_general(
            (plus - minus).astype(bf16), sin_table, contract, preferred_element_type=jnp.float32
        )
        real = scale * (even * cos_c - odd * sin_c)
        imag = scale * (even * sin_c + odd * cos_c)
        shares = jnp.stack([real, imag], 1).reshape(rows, 2, total, slot_count).transpose(2, 0, 1, 3)
        shares = shares.reshape(total, rows, lanes)
        tail = jnp.broadcast_to(split_scalar(partial, (pad_rows, lanes)), (total, pad_rows, lanes))
        messages = jnp.concatenate([shares, tail], 1).astype(bf16)
        arrived = exchange(messages, blk_count, quarter_count, False).astype(jnp.float32)
        summed = jnp.sum(arrived[:, rows:])
        returned = jnp.sum(arrived[:, :rows].reshape(blk_count, quarter_count, rows, lanes), 1)
        return to_coefficients(returned), summed

    def to_coefficients(returned):
        returned = returned.reshape(blk_count, funcs, cycle_local // 2, 2, 2, slot_count)
        north, south = returned[:, :, :, 0], returned[:, :, :, 1]
        combined = jnp.stack([north + south, north - south], 0).astype(bf16)
        combined = combined.transpose(5, 0, 4, 2, 1, 3).reshape(slot_count, 2, 2, funcs, cycle_pairs)
        parts = jnp.einsum("sjl,sucfj->sucfl", legendre, combined, preferred_element_type=jnp.float32)
        picked = jnp.where(even_mask, parts[:, 0], parts[:, 1])
        return jnp.sum(degree_gain[None, None, :, :] * picked, 2)

    zero = jnp.float32(0.0)
    one = jnp.float32(1.0)
    solution = start
    if fused:
        stacked_weight = jnp.concatenate([weight_plus, weight_minus], 0)
        image = jnp.concatenate([observed_plus, observed_minus], 0)
        legendre_rows = legendre.transpose(1, 0, 2).reshape(cycle_pairs * slot_count, degree_count)
        order_sign = (1 - 2 * (my_orders % 2)).astype(jnp.float32)
        order_sign = jnp.concatenate([order_sign, order_sign])[:, None]
        factor = precondition[None, :]

        def stage(factors, coefficients, multiplier, old):
            params = jnp.broadcast_to(jnp.stack(factors + [zero] * 4)[:, None], (8, lanes))
            messages = synth_stage(
                coefficients, multiplier, degree_gain, order_sign, legendre_rows, blk_count
            )
            returned, image, sums = grid_stage(
                params, messages, old, stacked_weight,
                cos_rot, sin_rot, table, blk_count, quarter_count, scale,
            )
            change = adjoint_stage(returned, degree_gain, order_sign, legendre_rows)
            return change, image, sums[0, 0], sums[1, 0]

        solution = start.transpose(1, 0, 2).reshape(lanes, degree_count)
        gradient, _, _, _ = stage([-one, one, zero, one], solution, jnp.ones_like(factor), image)
        direction = energy = None
        for iteration in range(ITERS):
            scaled_grad = factor * gradient
            factors = [one, zero, zero, one] if iteration == 0 else [one, zero, one, energy]
            change, image, energy_next, curvature = stage(factors, gradient, factor, image)
            if iteration == 0:
                direction = scaled_grad
            else:
                direction = scaled_grad + energy_next / energy * direction
            energy = energy_next
            step_size = energy / curvature
            solution = solution + step_size * direction
            gradient = gradient - step_size * change
        return tuple(
            out.reshape(2, slot_count, degree_count).transpose(1, 0, 2) for out in (solution, gradient)
        )
    plus, minus, _ = to_grid(start, zero)
    gradient, _ = to_orders(
        weight_plus * (observed_plus - plus), weight_minus * (observed_minus - minus), zero
    )
    direction = energy = image = None
    for iteration in range(ITERS):
        scaled_grad = precondition * gradient
        plus, minus, energy_next = to_grid(scaled_grad, jnp.sum(gradient * scaled_grad))
        if iteration == 0:
            direction = scaled_grad
        else:
            ratio = energy_next / energy
            direction = scaled_grad + ratio * direction
            plus = plus + ratio * image[0]
            minus = minus + ratio * image[1]
        image = (plus, minus)
        energy = energy_next
        weighted_plus, weighted_minus = weight_plus * plus, weight_minus * minus
        partial = jnp.sum(weighted_plus * plus + weighted_minus * minus)
        change, curvature = to_orders(weighted_plus, weighted_minus, partial)
        step_size = energy / curvature
        solution = solution + step_size * direction
        gradient = gradient - step_size * change
    return (solution, gradient)


def solution(mesh):
    return jax.shard_map(
        body,
        mesh=mesh,
        in_specs=(
            P(("blk", "quarter"), None, None),
            P(None, "blk", "quarter"),
            P(None, "blk", "quarter"),
            P(),
            P(),
            P(("blk", "quarter"), None, None),
            P(),
        ),
        out_specs=(P(("blk", "quarter"), None, None), P(("blk", "quarter"), None, None)),
        check_vma=False,
    )
```

```python
import functools
import math

import jax
import jax.numpy as jnp
from jax import lax
from jax.experimental import pallas as pl
from jax.experimental.pallas import tpu as pltpu
from jax.sharding import PartitionSpec as P

ITERS = 2
MESH = pl.DeviceIdType.MESH


def exchange_kernel(blk_count, quarter_count, per_blk, send_ref, recv_ref, send_sem, recv_sem):
    total = blk_count * quarter_count
    blk = lax.axis_index("blk")
    quarter = lax.axis_index("quarter")
    me = blk * quarter_count + quarter
    barrier = pltpu.get_barrier_semaphore()

    def greet(i, carry):
        peer = lax.rem(me + i, total)
        pl.semaphore_signal(
            barrier,
            inc=1,
            device_id=(lax.div(peer, quarter_count), lax.rem(peer, quarter_count)),
            device_id_type=MESH,
        )
        return carry

    lax.fori_loop(1, total, greet, 0)
    recv_ref[me] = send_ref[blk if per_blk else me]
    pl.semaphore_wait(barrier, total - 1)

    def send(i, carry):
        peer = lax.rem(me + i, total)
        peer_blk = lax.div(peer, quarter_count)
        pltpu.make_async_remote_copy(
            src_ref=send_ref.at[peer_blk if per_blk else peer],
            dst_ref=recv_ref.at[me],
            send_sem=send_sem,
            recv_sem=recv_sem,
            device_id=(peer_blk, lax.rem(peer, quarter_count)),
            device_id_type=MESH,
        ).start()
        return carry

    lax.fori_loop(1, total, send, 0)
    landed = recv_ref.at[pl.ds(0, total - 1)]
    pltpu.make_async_copy(landed, landed, recv_sem).wait()
    pltpu.make_async_copy(landed, landed, send_sem).wait()


def exchange(messages, blk_count, quarter_count, per_blk):
    total = blk_count * quarter_count
    return pl.pallas_call(
        functools.partial(exchange_kernel, blk_count, quarter_count, per_blk),
        out_shape=jax.ShapeDtypeStruct((total,) + messages.shape[1:], messages.dtype),
        in_specs=[pl.BlockSpec(memory_space=pltpu.VMEM)],
        out_specs=pl.BlockSpec(memory_space=pltpu.VMEM),
        scratch_shapes=[pltpu.SemaphoreType.DMA(()), pltpu.SemaphoreType.DMA(())],
        compiler_params=pltpu.CompilerParams(
            collective_id=0 if per_blk else 1, has_side_effects=True, vmem_limit_bytes=32 << 20
        ),
        name="to_cycles" if per_blk else "to_orders",
    )(messages)


def peers(blk_count, quarter_count, act):
    blk = lax.axis_index("blk")
    quarter = lax.axis_index("quarter")
    quarters = [lax.rem(quarter + i, quarter_count) for i in range(quarter_count)]
    for other in quarters[1:]:
        act(blk, other)

    def visit(i, carry):
        other_blk = lax.rem(blk + i, blk_count)
        for other in quarters:
            act(other_blk, other)
        return carry

    lax.fori_loop(1, blk_count, visit, 0)


def scatter(me, blk_count, quarter_count, send_ref, recv_ref, send_sem, recv_sem):
    def send(peer_blk, peer_quarter):
        pltpu.make_async_remote_copy(
            src_ref=send_ref.at[peer_blk],
            dst_ref=recv_ref.at[me],
            send_sem=send_sem,
            recv_sem=recv_sem,
            device_id=(peer_blk, peer_quarter),
            device_id_type=MESH,
        ).start()

    peers(blk_count, quarter_count, send)


def grid_kernel(
    blk_count,
    quarter_count,
    scale,
    params_ref,
    send_ref,
    old_ref,
    weight_ref,
    cos_ref,
    sin_ref,
    table_ref,
    returned_ref,
    image_ref,
    sums_ref,
    arrived_ref,
    left_ref,
    shares_ref,
    landed_ref,
    send_sem,
    recv_sem,
):
    total = blk_count * quarter_count
    blk = lax.axis_index("blk")
    quarter = lax.axis_index("quarter")
    me = blk * quarter_count + quarter
    barrier = pltpu.get_barrier_semaphore()

    def greet(peer_blk, peer_quarter):
        pl.semaphore_signal(
            barrier, inc=1, device_id=(peer_blk, peer_quarter), device_id_type=MESH
        )

    peers(blk_count, quarter_count, greet)
    arrived_ref[me] = send_ref[blk]
    pl.semaphore_wait(barrier, total - 1)
    scatter(me, blk_count, quarter_count, send_ref, arrived_ref, send_sem.at[0], recv_sem.at[0])
    some = arrived_ref.at[pl.ds(0, total - 1)]
    pltpu.make_async_copy(some, some, recv_sem.at[0]).wait()

    arrived = arrived_ref[...].astype(jnp.float32)
    rows = arrived.shape[1] // 2
    lanes = arrived.shape[2]
    lane = lax.broadcasted_iota(jnp.int32, (1, 1, lanes), 2)
    sign = jnp.where(lane < lanes // 2, jnp.float32(1.0), jnp.float32(-1.0))
    values = arrived[:, :rows]
    turned = values * cos_ref[...] + pltpu.roll(values, lanes // 2, 2) * sin_ref[...]
    left = jnp.concatenate([turned, turned * sign], 1).astype(jnp.bfloat16)
    for d in range(total):
        left_ref[:, d * lanes : (d + 1) * lanes] = left[d]
    tail = jnp.sum(arrived[:, rows:], 0)
    energy = jnp.sum(jnp.sum(tail, 1, keepdims=True), 0, keepdims=True)

    field = scale * jnp.dot(left_ref[...], table_ref[...], preferred_element_type=jnp.float32)
    params = params_ref[...]
    ratio = params[1:2, 0:1] + params[2:3, 0:1] * energy / params[3:4, 0:1]
    image = params[0:1, 0:1] * field + ratio * old_ref[...]
    image_ref[...] = image
    weighted = weight_ref[...] * image
    partial = jnp.sum(weighted * image, 0, keepdims=True)
    partial = sum(partial[:, i : i + lanes] for i in range(0, partial.shape[1], lanes))
    high = partial.astype(jnp.bfloat16).astype(jnp.float32)
    middle = (partial - high).astype(jnp.bfloat16).astype(jnp.float32)
    low = partial - high - middle
    row = lax.broadcasted_iota(jnp.int32, (rows, lanes), 0)
    tail = jnp.where(row == 0, high, jnp.where(row == 1, middle, jnp.where(row == 2, low, 0.0)))
    plus, minus = weighted[:rows], weighted[rows:]
    folded = jnp.concatenate([plus + minus, plus - minus], 0).astype(jnp.bfloat16)
    cos_lanes = lax.broadcasted_iota(jnp.int32, (rows, lanes), 1) < lanes // 2
    width = quarter_count * lanes
    quarters = [lax.rem(quarter + i, quarter_count) for i in range(quarter_count)]
    for i in range(1, blk_count + 1):
        chunk = lax.rem(blk + i, blk_count)
        back = lax.dot_general(
            folded,
            table_ref[pl.ds(pl.multiple_of(chunk * width, width), width), :],
            (((1,), (1,)), ((), ())),
            preferred_element_type=jnp.float32,
        )
        for q in range(quarter_count):
            d = chunk * quarter_count + q
            part = back[:, q * lanes : (q + 1) * lanes]
            picked = scale * jnp.where(cos_lanes, part[:rows], part[rows:])
            share = picked * cos_ref[d] - pltpu.roll(picked, lanes // 2, 1) * sin_ref[d]
            shares_ref[d] = jnp.concatenate([share, tail], 0).astype(jnp.bfloat16)
        for other in quarters[1:] if i == blk_count else quarters:
            pltpu.make_async_remote_copy(
                src_ref=shares_ref.at[chunk * quarter_count + other],
                dst_ref=landed_ref.at[me],
                send_sem=send_sem.at[1],
                recv_sem=recv_sem.at[1],
                device_id=(chunk, other),
                device_id_type=MESH,
            ).start()

    landed_ref[me] = shares_ref[me]
    some = landed_ref.at[pl.ds(0, total - 1)]
    pltpu.make_async_copy(some, some, recv_sem.at[1]).wait()
    landed = landed_ref[...].astype(jnp.float32)
    for b in range(blk_count):
        returned_ref[b] = sum(landed[b * quarter_count + q, :rows] for q in range(quarter_count))
    tail = jnp.sum(landed[:, rows:], 0)
    curvature = jnp.sum(jnp.sum(tail, 1, keepdims=True), 0, keepdims=True)
    sums_ref[...] = jnp.where(row == 0, energy, curvature)
    pltpu.make_async_copy(some, some, send_sem.at[0]).wait()
    pltpu.make_async_copy(some, some, send_sem.at[1]).wait()


def grid_stage(params, messages, old, weight, cos_rot, sin_rot, table, blk_count, quarter_count, scale):
    total = blk_count * quarter_count
    block_rows, lanes = messages.shape[1:]
    rows = block_rows // 2
    block = (total, block_rows, lanes)
    return pl.pallas_call(
        functools.partial(grid_kernel, blk_count, quarter_count, scale),
        out_shape=(
            jax.ShapeDtypeStruct((blk_count, rows, lanes), jnp.float32),
            jax.ShapeDtypeStruct(old.shape, jnp.float32),
            jax.ShapeDtypeStruct((rows, lanes), jnp.float32),
        ),
        in_specs=[pl.BlockSpec(memory_space=pltpu.VMEM)] * 7,
        out_specs=(pl.BlockSpec(memory_space=pltpu.VMEM),) * 3,
        scratch_shapes=[
            pltpu.VMEM(block, jnp.bfloat16),
            pltpu.VMEM((block_rows, total * lanes), jnp.bfloat16),
            pltpu.VMEM(block, jnp.bfloat16),
            pltpu.VMEM(block, jnp.bfloat16),
            pltpu.SemaphoreType.DMA((2,)),
            pltpu.SemaphoreType.DMA((2,)),
        ],
        compiler_params=pltpu.CompilerParams(
            collective_id=2, has_side_effects=True, vmem_limit_bytes=14 << 20
        ),
        name="grid_stage",
    )(params, messages, old, weight, cos_rot, sin_rot, table)


def synth_kernel(
    blk_count, values_ref, factor_ref, gain_ref, sign_ref, legendre_ref, message_ref, right_ref, rows_ref
):
    lanes, degree_count = values_ref.shape
    slot_count = lanes // 2
    funcs = gain_ref.shape[0]
    values = values_ref[...]
    scaled = factor_ref[...] * values
    lane_sign = 1 - 2 * (lax.broadcasted_iota(jnp.int32, (1, degree_count), 1) % 2)
    sign = sign_ref[...] * lane_sign.astype(jnp.float32)
    partial = jnp.sum(values * scaled, 0, keepdims=True)
    partial = sum(partial[:, i : i + lanes] for i in range(0, degree_count, lanes))
    high = partial.astype(jnp.bfloat16).astype(jnp.float32)
    middle = (partial - high).astype(jnp.bfloat16).astype(jnp.float32)
    low = partial - high - middle
    row = lax.broadcasted_iota(jnp.int32, (8, lanes), 0)
    tail = jnp.where(row == 0, high, jnp.where(row == 1, middle, jnp.where(row == 2, low, 0.0)))
    slot = lax.broadcasted_iota(jnp.int32, (slot_count, 2 * lanes), 0)
    lane = lax.broadcasted_iota(jnp.int32, (slot_count, 2 * lanes), 1)
    own = slot == lane % slot_count
    for f in range(funcs):
        north = gain_ref[f : f + 1, :] * scaled
        right_ref[:lanes] = north.astype(jnp.bfloat16)
        right_ref[lanes:] = (north * sign).astype(jnp.bfloat16)
        parts = lax.dot_general(
            legendre_ref[...], right_ref[...], (((1,), (1,)), ((), ())),
            preferred_element_type=jnp.float32,
        )
        for j in range(blk_count):
            part = parts[j * slot_count : (j + 1) * slot_count]
            kept = jnp.sum(jnp.where(own, part, 0.0), 0, keepdims=True)
            rows_ref[j, 2 * f : 2 * f + 1, :] = kept[:, :lanes]
            rows_ref[j, 2 * f + 1 : 2 * f + 2, :] = kept[:, lanes:]
    for j in range(blk_count):
        message_ref[j] = jnp.concatenate([rows_ref[j], tail], 0).astype(jnp.bfloat16)


def synth_stage(values, factor, gains, sign, legendre_rows, blk_count):
    lanes, degree_count = values.shape
    rows = 2 * gains.shape[0]
    return pl.pallas_call(
        functools.partial(synth_kernel, blk_count),
        out_shape=jax.ShapeDtypeStruct((blk_count, 2 * rows, lanes), jnp.bfloat16),
        in_specs=[pl.BlockSpec(memory_space=pltpu.VMEM)] * 5,
        out_specs=pl.BlockSpec(memory_space=pltpu.VMEM),
        scratch_shapes=[
            pltpu.VMEM((2 * lanes, degree_count), jnp.bfloat16),
            pltpu.VMEM((blk_count, rows, lanes), jnp.float32),
        ],
        compiler_params=pltpu.CompilerParams(vmem_limit_bytes=14 << 20),
        name="synth_stage",
    )(values, factor, gains, sign, legendre_rows)


def adjoint_kernel(blk_count, returned_ref, gain_ref, sign_ref, legendre_ref, change_ref, left_ref):
    lanes, degree_count = change_ref.shape
    slot_count = lanes // 2
    funcs = gain_ref.shape[0]
    slot = lax.broadcasted_iota(jnp.int32, (slot_count, lanes), 0)
    lane = lax.broadcasted_iota(jnp.int32, (slot_count, lanes), 1)
    own = slot == lane % slot_count
    first = lax.broadcasted_iota(jnp.int32, (1, lanes), 1) < slot_count
    for a in range(blk_count // 2):
        near, far = returned_ref[2 * a], returned_ref[2 * a + 1]
        near_turned, far_turned = pltpu.roll(near, slot_count, 1), pltpu.roll(far, slot_count, 1)
        parts = (jnp.where(first, near, far_turned), jnp.where(first, near_turned, far))
        for c in range(2):
            for f in range(funcs):
                north = parts[c][2 * f : 2 * f + 1]
                south = parts[c][2 * f + 1 : 2 * f + 2]
                for u, hemis in enumerate((north + south, north - south)):
                    at = ((c * funcs + f) * 2 + u) * slot_count
                    left_ref[at : at + slot_count, a * lanes : (a + 1) * lanes] = jnp.where(
                        own, hemis, 0.0
                    ).astype(jnp.bfloat16)
    width = 256
    even_lane = lax.broadcasted_iota(jnp.int32, (slot_count, width), 1) % 2 == 0
    even_order = sign_ref[:slot_count, :] > 0.0
    even = even_lane == even_order
    for at in range(0, degree_count, width):
        parts = jnp.dot(
            left_ref[...], legendre_ref[:, at : at + width], preferred_element_type=jnp.float32
        )
        for c in range(2):
            total = None
            for f in range(funcs):
                base = (c * funcs + f) * 2 * slot_count
                picked = jnp.where(
                    even, parts[base : base + slot_count],
                    parts[base + slot_count : base + 2 * slot_count],
                )
                term = gain_ref[f : f + 1, at : at + width] * picked
                total = term if f == 0 else total + term
            change_ref[c * slot_count : (c + 1) * slot_count, at : at + width] = total


def adjoint_stage(returned, gains, sign, legendre_rows):
    blk_count, rows, lanes = returned.shape
    degree_count = legendre_rows.shape[1]
    return pl.pallas_call(
        functools.partial(adjoint_kernel, blk_count),
        out_shape=jax.ShapeDtypeStruct((lanes, degree_count), jnp.float32),
        in_specs=[pl.BlockSpec(memory_space=pltpu.VMEM)] * 4,
        out_specs=pl.BlockSpec(memory_space=pltpu.VMEM),
        scratch_shapes=[pltpu.VMEM((rows * lanes, legendre_rows.shape[0]), jnp.bfloat16)],
        compiler_params=pltpu.CompilerParams(vmem_limit_bytes=14 << 20),
        name="adjoint_stage",
    )(returned, gains, sign, legendre_rows)


def half_turn_sine(phase, quarter_turn):
    z = phase.astype(jnp.float32) * (1.0 / quarter_turn)
    y = z * z
    acc = jnp.float32(-3.41817280e-06)
    for coef in (1.60217136e-04, -4.68162024e-03, 7.96925873e-02, -6.45964093e-01, 1.57079633):
        acc = acc * y + jnp.float32(coef)
    return acc * z


def table_kernel(total, order_ref, table_ref):
    rows, half_lon = table_ref.shape
    slot_count = rows // total // 2
    period = 4 * half_lon * lax.axis_size("quarter")
    lane = lax.broadcasted_iota(jnp.int32, (slot_count, 128), 1)
    fine = (2 * lane + 1).astype(jnp.float32)
    coarse = (256 * jnp.minimum(lane, half_lon // 128)).astype(jnp.float32)

    def fill(d, carry):
        orders = order_ref[pl.ds(pl.multiple_of(d * slot_count, slot_count), slot_count), :]
        orders = orders.astype(jnp.float32)
        cos_b, sin_b = cos_sin((orders * fine).astype(jnp.int32), period)
        cos_a, sin_a = cos_sin((orders * coarse).astype(jnp.int32), period)
        at = pl.multiple_of(d * 2 * slot_count, 2 * slot_count)
        for i in range(half_lon // 128):
            cos_i, sin_i = cos_a[:, i : i + 1], sin_a[:, i : i + 1]
            lon = slice(i * 128, (i + 1) * 128)
            cosine = cos_i * cos_b - sin_i * sin_b
            sine = sin_i * cos_b + cos_i * sin_b
            table_ref[pl.ds(at, 2 * slot_count), lon] = jnp.concatenate([cosine, sine], 0).astype(
                jnp.bfloat16
            )
        return carry

    lax.fori_loop(0, total, fill, 0, unroll=2)


def table_stage(orders, total, half_lon):
    return pl.pallas_call(
        functools.partial(table_kernel, total),
        out_shape=jax.ShapeDtypeStruct((2 * orders.shape[0], half_lon), jnp.bfloat16),
        in_specs=[pl.BlockSpec(memory_space=pltpu.VMEM)],
        out_specs=pl.BlockSpec(memory_space=pltpu.VMEM),
        compiler_params=pltpu.CompilerParams(vmem_limit_bytes=14 << 20),
        name="table_stage",
    )(orders)


def cos_sin(steps, period):
    turn = jnp.bitwise_and(steps, period - 1)
    half = period // 2
    quarter = period // 4
    cosine = half_turn_sine(jnp.abs(turn - half) - quarter, quarter)
    shifted = jnp.bitwise_and(turn - quarter, period - 1)
    sine = half_turn_sine(jnp.abs(shifted - half) - quarter, quarter)
    return cosine, sine


def split_scalar(value, shape):
    hi = lax.reduce_precision(value, 8, 7)
    mid = lax.reduce_precision(value - hi, 8, 7)
    low = value - hi - mid
    lane = lax.broadcasted_iota(jnp.int32, shape, len(shape) - 1)
    zero = jnp.float32(0.0)
    picked = jnp.where(lane == 0, hi, jnp.where(lane == 1, mid, jnp.where(lane == 2, low, zero)))
    row = lax.broadcasted_iota(jnp.int32, shape, len(shape) - 2)
    return jnp.where(row == 0, picked, zero)


def body(start, observed, coverage, class_weight, degree_gain, legendre, order_table):
    blk_count = lax.axis_size("blk")
    quarter_count = lax.axis_size("quarter")
    blk_index = lax.axis_index("blk")
    quarter_index = lax.axis_index("quarter")
    total = blk_count * quarter_count
    slot_count, cycle_pairs, degree_count = legendre.shape
    order_count = order_table.shape[0]
    funcs, cycle_local, lon_local = observed.shape
    lon_total = lon_local * quarter_count
    half_lon = lon_local // 2
    rows = funcs * cycle_local
    lanes = 2 * slot_count
    pad_rows = -(rows + 1) % 16 + 1
    scale = lon_total ** (-0.5)
    bf16 = jnp.bfloat16
    first_slot = (blk_index * quarter_count + quarter_index) * slot_count
    my_orders = lax.dynamic_slice_in_dim(order_table, first_slot, slot_count)

    fused = lanes == 128 and rows == 8 and cycle_local == 2 and cycle_pairs == blk_count and half_lon % 128 == 0
    centre = 2 * lon_local * quarter_index + (lon_local - 1)
    cos_c, sin_c = cos_sin(order_table * centre, 2 * lon_total)
    if fused:
        table = table_stage(order_table[:, None], total, half_lon)
        cos_c = cos_c.reshape(total, 1, slot_count)
        sin_c = sin_c.reshape(total, 1, slot_count)
        cos_rot = jnp.concatenate([cos_c, cos_c], 2)
        sin_rot = jnp.concatenate([sin_c, -sin_c], 2)
    else:
        tile = min(128, half_lon)
        coarse = jnp.arange(half_lon // tile, dtype=jnp.int32) * tile
        fine = 2 * jnp.arange(tile, dtype=jnp.int32) + 1
        cos_a, sin_a = cos_sin(order_table[:, None] * (2 * coarse)[None, :], 2 * lon_total)
        cos_b, sin_b = cos_sin(order_table[:, None] * fine[None, :], 2 * lon_total)
        cos_a, sin_a, cos_b, sin_b, cos_c, sin_c = lax.optimization_barrier(
            (cos_a, sin_a, cos_b, sin_b, cos_c, sin_c)
        )
        cos_table = jnp.concatenate(
            [cos_a[:, i : i + 1] * cos_b - sin_a[:, i : i + 1] * sin_b for i in range(coarse.shape[0])], 1
        ).astype(bf16)
        sin_table = jnp.concatenate(
            [sin_a[:, i : i + 1] * cos_b + cos_a[:, i : i + 1] * sin_b for i in range(coarse.shape[0])], 1
        ).astype(bf16)

    pair_index = blk_index * (cycle_local // 2) + jnp.arange(cycle_local // 2, dtype=jnp.int32)
    theta = (pair_index.astype(jnp.float32) + 0.5) * (math.pi / (2 * cycle_pairs))
    area = jnp.repeat(jnp.sin(theta), 2)
    classes = jnp.arange(1, class_weight.shape[1] + 1, dtype=jnp.int32)
    matched = coverage[..., None] == classes
    cell_weight = jnp.sum(jnp.where(matched, class_weight[:, None, None, :], 0.0), -1)
    weight = (cell_weight * area[None, :, None]).reshape(rows, lon_local)

    def fold(grid):
        return grid[:, half_lon:], jnp.flip(grid[:, :half_lon], 1)

    observed_plus, observed_minus = fold(observed.reshape(rows, lon_local))
    weight_plus, weight_minus = fold(weight)
    precondition = 1.0 / (jnp.arange(degree_count, dtype=jnp.int32).astype(jnp.float32) + 1.0)

    degrees = jnp.arange(degree_count, dtype=jnp.int32)
    even_mask = ((degrees[None, :] + my_orders[:, None]) % 2 == 0)[:, None, None, :]

    def to_messages(coefficients, partial):
        scaled = degree_gain[None, :, None, :] * coefficients[:, None]
        zeros = jnp.zeros_like(scaled)
        parity = jnp.stack(
            [jnp.where(even_mask, scaled, zeros), jnp.where(even_mask, zeros, scaled)], 1
        ).astype(bf16)
        parts = jnp.einsum("sjl,stfcl->tjfcs", legendre, parity, preferred_element_type=jnp.float32)
        spectra = jnp.stack([parts[0] + parts[1], parts[0] - parts[1]], 1)
        spectra = spectra.reshape(blk_count, cycle_local, funcs, lanes).transpose(0, 2, 1, 3)
        spectra = spectra.reshape(blk_count, rows, lanes)
        tail = jnp.broadcast_to(split_scalar(partial, (pad_rows, lanes)), (blk_count, pad_rows, lanes))
        return jnp.concatenate([spectra, tail], 1).astype(bf16)

    def to_grid(coefficients, partial):
        messages = to_messages(coefficients, partial)
        arrived = exchange(messages, blk_count, quarter_count, True).astype(jnp.float32)
        summed = jnp.sum(arrived[:, rows:])
        spectra = arrived[:, :rows].reshape(total, rows, 2, slot_count).transpose(2, 1, 0, 3)
        spectra = spectra.reshape(2, rows, order_count)
        real = (spectra[0] * cos_c + spectra[1] * sin_c).astype(bf16)
        imag = (spectra[1] * cos_c - spectra[0] * sin_c).astype(bf16)
        even = scale * jnp.dot(real, cos_table, preferred_element_type=jnp.float32)
        odd = scale * jnp.dot(imag, sin_table, preferred_element_type=jnp.float32)
        return even + odd, even - odd, summed

    def to_orders(plus, minus, partial):
        contract = (((1,), (1,)), ((), ()))
        even = lax.dot_general(
            (plus + minus).astype(bf16), cos_table, contract, preferred_element_type=jnp.float32
        )
        odd = lax.dot_general(
            (plus - minus).astype(bf16), sin_table, contract, preferred_element_type=jnp.float32
        )
        real = scale * (even * cos_c - odd * sin_c)
        imag = scale * (even * sin_c + odd * cos_c)
        shares = jnp.stack([real, imag], 1).reshape(rows, 2, total, slot_count).transpose(2, 0, 1, 3)
        shares = shares.reshape(total, rows, lanes)
        tail = jnp.broadcast_to(split_scalar(partial, (pad_rows, lanes)), (total, pad_rows, lanes))
        messages = jnp.concatenate([shares, tail], 1).astype(bf16)
        arrived = exchange(messages, blk_count, quarter_count, False).astype(jnp.float32)
        summed = jnp.sum(arrived[:, rows:])
        returned = jnp.sum(arrived[:, :rows].reshape(blk_count, quarter_count, rows, lanes), 1)
        return to_coefficients(returned), summed

    def to_coefficients(returned):
        returned = returned.reshape(blk_count, funcs, cycle_local // 2, 2, 2, slot_count)
        north, south = returned[:, :, :, 0], returned[:, :, :, 1]
        combined = jnp.stack([north + south, north - south], 0).astype(bf16)
        combined = combined.transpose(5, 0, 4, 2, 1, 3).reshape(slot_count, 2, 2, funcs, cycle_pairs)
        parts = jnp.einsum("sjl,sucfj->sucfl", legendre, combined, preferred_element_type=jnp.float32)
        picked = jnp.where(even_mask, parts[:, 0], parts[:, 1])
        return jnp.sum(degree_gain[None, None, :, :] * picked, 2)

    zero = jnp.float32(0.0)
    one = jnp.float32(1.0)
    solution = start
    if fused:
        stacked_weight = jnp.concatenate([weight_plus, weight_minus], 0)
        image = jnp.concatenate([observed_plus, observed_minus], 0)
        legendre_rows = legendre.transpose(1, 0, 2).reshape(cycle_pairs * slot_count, degree_count)
        order_sign = (1 - 2 * (my_orders % 2)).astype(jnp.float32)
        order_sign = jnp.concatenate([order_sign, order_sign])[:, None]
        factor = precondition[None, :]

        def stage(factors, coefficients, multiplier, old):
            params = jnp.broadcast_to(jnp.stack(factors + [zero] * 4)[:, None], (8, lanes))
            messages = synth_stage(
                coefficients, multiplier, degree_gain, order_sign, legendre_rows, blk_count
            )
            returned, image, sums = grid_stage(
                params, messages, old, stacked_weight,
                cos_rot, sin_rot, table, blk_count, quarter_count, scale,
            )
            change = adjoint_stage(returned, degree_gain, order_sign, legendre_rows)
            return change, image, sums[0, 0], sums[1, 0]

        solution = start.transpose(1, 0, 2).reshape(lanes, degree_count)
        gradient, _, _, _ = stage([-one, one, zero, one], solution, jnp.ones_like(factor), image)
        direction = energy = None
        for iteration in range(ITERS):
            scaled_grad = factor * gradient
            factors = [one, zero, zero, one] if iteration == 0 else [one, zero, one, energy]
            change, image, energy_next, curvature = stage(factors, gradient, factor, image)
            if iteration == 0:
                direction = scaled_grad
            else:
                direction = scaled_grad + energy_next / energy * direction
            energy = energy_next
            step_size = energy / curvature
            solution = solution + step_size * direction
            gradient = gradient - step_size * change
        return tuple(
            out.reshape(2, slot_count, degree_count).transpose(1, 0, 2) for out in (solution, gradient)
        )
    plus, minus, _ = to_grid(start, zero)
    gradient, _ = to_orders(
        weight_plus * (observed_plus - plus), weight_minus * (observed_minus - minus), zero
    )
    direction = energy = image = None
    for iteration in range(ITERS):
        scaled_grad = precondition * gradient
        plus, minus, energy_next = to_grid(scaled_grad, jnp.sum(gradient * scaled_grad))
        if iteration == 0:
            direction = scaled_grad
        else:
            ratio = energy_next / energy
            direction = scaled_grad + ratio * direction
            plus = plus + ratio * image[0]
            minus = minus + ratio * image[1]
        image = (plus, minus)
        energy = energy_next
        weighted_plus, weighted_minus = weight_plus * plus, weight_minus * minus
        partial = jnp.sum(weighted_plus * plus + weighted_minus * minus)
        change, curvature = to_orders(weighted_plus, weighted_minus, partial)
        step_size = energy / curvature
        solution = solution + step_size * direction
        gradient = gradient - step_size * change
    return (solution, gradient)


def solution(mesh):
    return jax.shard_map(
        body,
        mesh=mesh,
        in_specs=(
            P(("blk", "quarter"), None, None),
            P(None, "blk", "quarter"),
            P(None, "blk", "quarter"),
            P(),
            P(),
            P(("blk", "quarter"), None, None),
            P(),
        ),
        out_specs=(P(("blk", "quarter"), None, None), P(("blk", "quarter"), None, None)),
        check_vma=False,
    )
```

```python
import functools
import math

import jax
import jax.numpy as jnp
from jax import lax
from jax.experimental import pallas as pl
from jax.experimental.pallas import tpu as pltpu
from jax.sharding import PartitionSpec as P

ITERS = 2
MESH = pl.DeviceIdType.MESH


def exchange_kernel(blk_count, quarter_count, per_blk, send_ref, recv_ref, send_sem, recv_sem):
    total = blk_count * quarter_count
    blk = lax.axis_index("blk")
    quarter = lax.axis_index("quarter")
    me = blk * quarter_count + quarter
    barrier = pltpu.get_barrier_semaphore()

    def greet(i, carry):
        peer = lax.rem(me + i, total)
        pl.semaphore_signal(
            barrier,
            inc=1,
            device_id=(lax.div(peer, quarter_count), lax.rem(peer, quarter_count)),
            device_id_type=MESH,
        )
        return carry

    lax.fori_loop(1, total, greet, 0)
    recv_ref[me] = send_ref[blk if per_blk else me]
    pl.semaphore_wait(barrier, total - 1)

    def send(i, carry):
        peer = lax.rem(me + i, total)
        peer_blk = lax.div(peer, quarter_count)
        pltpu.make_async_remote_copy(
            src_ref=send_ref.at[peer_blk if per_blk else peer],
            dst_ref=recv_ref.at[me],
            send_sem=send_sem,
            recv_sem=recv_sem,
            device_id=(peer_blk, lax.rem(peer, quarter_count)),
            device_id_type=MESH,
        ).start()
        return carry

    lax.fori_loop(1, total, send, 0)
    landed = recv_ref.at[pl.ds(0, total - 1)]
    pltpu.make_async_copy(landed, landed, recv_sem).wait()
    pltpu.make_async_copy(landed, landed, send_sem).wait()


def exchange(messages, blk_count, quarter_count, per_blk):
    total = blk_count * quarter_count
    return pl.pallas_call(
        functools.partial(exchange_kernel, blk_count, quarter_count, per_blk),
        out_shape=jax.ShapeDtypeStruct((total,) + messages.shape[1:], messages.dtype),
        in_specs=[pl.BlockSpec(memory_space=pltpu.VMEM)],
        out_specs=pl.BlockSpec(memory_space=pltpu.VMEM),
        scratch_shapes=[pltpu.SemaphoreType.DMA(()), pltpu.SemaphoreType.DMA(())],
        compiler_params=pltpu.CompilerParams(
            collective_id=0 if per_blk else 1, has_side_effects=True, vmem_limit_bytes=32 << 20
        ),
        name="to_cycles" if per_blk else "to_orders",
    )(messages)


def peers(blk_count, quarter_count, act):
    blk = lax.axis_index("blk")
    quarter = lax.axis_index("quarter")
    quarters = [lax.rem(quarter + i, quarter_count) for i in range(quarter_count)]
    for other in quarters[1:]:
        act(blk, other)

    def visit(i, carry):
        other_blk = lax.rem(blk + i, blk_count)
        for other in quarters:
            act(other_blk, other)
        return carry

    lax.fori_loop(1, blk_count, visit, 0)


def scatter(me, blk_count, quarter_count, send_ref, recv_ref, send_sem, recv_sem):
    def send(peer_blk, peer_quarter):
        pltpu.make_async_remote_copy(
            src_ref=send_ref.at[peer_blk],
            dst_ref=recv_ref.at[me],
            send_sem=send_sem,
            recv_sem=recv_sem,
            device_id=(peer_blk, peer_quarter),
            device_id_type=MESH,
        ).start()

    peers(blk_count, quarter_count, send)


def grid_kernel(
    blk_count,
    quarter_count,
    scale,
    params_ref,
    send_ref,
    old_ref,
    weight_ref,
    cos_ref,
    sin_ref,
    table_ref,
    returned_ref,
    image_ref,
    sums_ref,
    arrived_ref,
    shares_ref,
    landed_ref,
    send_sem,
    recv_sem,
    arrive_sem,
):
    total = blk_count * quarter_count
    blk = lax.axis_index("blk")
    quarter = lax.axis_index("quarter")
    me = blk * quarter_count + quarter
    barrier = pltpu.get_barrier_semaphore()

    def greet(peer_blk, peer_quarter):
        pl.semaphore_signal(
            barrier, inc=1, device_id=(peer_blk, peer_quarter), device_id_type=MESH
        )

    peers(blk_count, quarter_count, greet)
    arrived_ref[me] = send_ref[blk]
    pl.semaphore_wait(barrier, total - 1)
    scatter(
        me, blk_count, quarter_count, send_ref, arrived_ref, send_sem.at[0], arrive_sem.at[blk]
    )
    rows, lanes = arrived_ref.shape[1] // 2, arrived_ref.shape[2]
    width = quarter_count * lanes
    lane = lax.broadcasted_iota(jnp.int32, (1, 1, lanes), 2)
    sign = jnp.where(lane < lanes // 2, jnp.float32(1.0), jnp.float32(-1.0))
    field = jnp.zeros(image_ref.shape, jnp.float32)
    tail = jnp.zeros((rows, lanes), jnp.float32)
    for i in range(blk_count):
        source = lax.rem(blk + blk_count - i, blk_count)
        base = source * quarter_count
        some = arrived_ref.at[pl.ds(base, quarter_count - 1 if i == 0 else quarter_count)]
        pltpu.make_async_copy(some, some, arrive_sem.at[source]).wait()
        near = pl.ds(base, quarter_count)
        arrived = arrived_ref[near].astype(jnp.float32)
        values = arrived[:, :rows]
        turned = values * cos_ref[near] + pltpu.roll(values, lanes // 2, 2) * sin_ref[near]
        left = jnp.concatenate([turned, turned * sign], 1).astype(jnp.bfloat16)
        field += jnp.dot(
            jnp.concatenate([left[q] for q in range(quarter_count)], 1),
            table_ref[pl.ds(pl.multiple_of(source * width, width), width), :],
            preferred_element_type=jnp.float32,
        )
        tail += jnp.sum(arrived[:, rows:], 0)
    energy = jnp.sum(jnp.sum(tail, 1, keepdims=True), 0, keepdims=True)
    field = scale * field
    params = params_ref[...]
    ratio = params[1:2, 0:1] + params[2:3, 0:1] * energy / params[3:4, 0:1]
    image = params[0:1, 0:1] * field + ratio * old_ref[...]
    image_ref[...] = image
    weighted = weight_ref[...] * image
    partial = jnp.sum(weighted * image, 0, keepdims=True)
    partial = sum(partial[:, i : i + lanes] for i in range(0, partial.shape[1], lanes))
    high = partial.astype(jnp.bfloat16).astype(jnp.float32)
    middle = (partial - high).astype(jnp.bfloat16).astype(jnp.float32)
    low = partial - high - middle
    row = lax.broadcasted_iota(jnp.int32, (rows, lanes), 0)
    tail = jnp.where(row == 0, high, jnp.where(row == 1, middle, jnp.where(row == 2, low, 0.0)))
    plus, minus = weighted[:rows], weighted[rows:]
    folded = jnp.concatenate([plus + minus, plus - minus], 0).astype(jnp.bfloat16)
    cos_lanes = lax.broadcasted_iota(jnp.int32, (rows, lanes), 1) < lanes // 2
    width = quarter_count * lanes
    quarters = [lax.rem(quarter + i, quarter_count) for i in range(quarter_count)]
    for i in range(1, blk_count + 1):
        chunk = lax.rem(blk + i, blk_count)
        back = lax.dot_general(
            folded,
            table_ref[pl.ds(pl.multiple_of(chunk * width, width), width), :],
            (((1,), (1,)), ((), ())),
            preferred_element_type=jnp.float32,
        )
        for q in range(quarter_count):
            d = chunk * quarter_count + q
            part = back[:, q * lanes : (q + 1) * lanes]
            picked = scale * jnp.where(cos_lanes, part[:rows], part[rows:])
            share = picked * cos_ref[d] - pltpu.roll(picked, lanes // 2, 1) * sin_ref[d]
            shares_ref[d] = jnp.concatenate([share, tail], 0).astype(jnp.bfloat16)
        for other in quarters[1:] if i == blk_count else quarters:
            pltpu.make_async_remote_copy(
                src_ref=shares_ref.at[chunk * quarter_count + other],
                dst_ref=landed_ref.at[me],
                send_sem=send_sem.at[1],
                recv_sem=recv_sem.at[1],
                device_id=(chunk, other),
                device_id_type=MESH,
            ).start()

    landed_ref[me] = shares_ref[me]
    some = landed_ref.at[pl.ds(0, total - 1)]
    pltpu.make_async_copy(some, some, recv_sem.at[1]).wait()
    landed = landed_ref[...].astype(jnp.float32)
    for b in range(blk_count):
        returned_ref[b] = sum(landed[b * quarter_count + q, :rows] for q in range(quarter_count))
    tail = jnp.sum(landed[:, rows:], 0)
    curvature = jnp.sum(jnp.sum(tail, 1, keepdims=True), 0, keepdims=True)
    sums_ref[...] = jnp.where(row == 0, energy, curvature)
    pltpu.make_async_copy(some, some, send_sem.at[0]).wait()
    pltpu.make_async_copy(some, some, send_sem.at[1]).wait()


def grid_stage(params, messages, old, weight, cos_rot, sin_rot, table, blk_count, quarter_count, scale):
    total = blk_count * quarter_count
    block_rows, lanes = messages.shape[1:]
    rows = block_rows // 2
    block = (total, block_rows, lanes)
    return pl.pallas_call(
        functools.partial(grid_kernel, blk_count, quarter_count, scale),
        out_shape=(
            jax.ShapeDtypeStruct((blk_count, rows, lanes), jnp.float32),
            jax.ShapeDtypeStruct(old.shape, jnp.float32),
            jax.ShapeDtypeStruct((rows, lanes), jnp.float32),
        ),
        in_specs=[pl.BlockSpec(memory_space=pltpu.VMEM)] * 7,
        out_specs=(pl.BlockSpec(memory_space=pltpu.VMEM),) * 3,
        scratch_shapes=[
            pltpu.VMEM(block, jnp.bfloat16),
            pltpu.VMEM(block, jnp.bfloat16),
            pltpu.VMEM(block, jnp.bfloat16),
            pltpu.SemaphoreType.DMA((2,)),
            pltpu.SemaphoreType.DMA((2,)),
            pltpu.SemaphoreType.DMA((blk_count,)),
        ],
        compiler_params=pltpu.CompilerParams(
            collective_id=2, has_side_effects=True, vmem_limit_bytes=14 << 20
        ),
        name="grid_stage",
    )(params, messages, old, weight, cos_rot, sin_rot, table)


def synth_kernel(
    blk_count, values_ref, factor_ref, gain_ref, sign_ref, legendre_ref, message_ref, right_ref, rows_ref
):
    lanes, degree_count = values_ref.shape
    slot_count = lanes // 2
    funcs = gain_ref.shape[0]
    values = values_ref[...]
    scaled = factor_ref[...] * values
    lane_sign = 1 - 2 * (lax.broadcasted_iota(jnp.int32, (1, degree_count), 1) % 2)
    sign = sign_ref[...] * lane_sign.astype(jnp.float32)
    partial = jnp.sum(values * scaled, 0, keepdims=True)
    partial = sum(partial[:, i : i + lanes] for i in range(0, degree_count, lanes))
    high = partial.astype(jnp.bfloat16).astype(jnp.float32)
    middle = (partial - high).astype(jnp.bfloat16).astype(jnp.float32)
    low = partial - high - middle
    row = lax.broadcasted_iota(jnp.int32, (8, lanes), 0)
    tail = jnp.where(row == 0, high, jnp.where(row == 1, middle, jnp.where(row == 2, low, 0.0)))
    slot = lax.broadcasted_iota(jnp.int32, (slot_count, 2 * lanes), 0)
    lane = lax.broadcasted_iota(jnp.int32, (slot_count, 2 * lanes), 1)
    own = slot == lane % slot_count
    for f in range(funcs):
        north = gain_ref[f : f + 1, :] * scaled
        right_ref[:lanes] = north.astype(jnp.bfloat16)
        right_ref[lanes:] = (north * sign).astype(jnp.bfloat16)
        parts = lax.dot_general(
            legendre_ref[...], right_ref[...], (((1,), (1,)), ((), ())),
            preferred_element_type=jnp.float32,
        )
        for j in range(blk_count):
            part = parts[j * slot_count : (j + 1) * slot_count]
            kept = jnp.sum(jnp.where(own, part, 0.0), 0, keepdims=True)
            rows_ref[j, 2 * f : 2 * f + 1, :] = kept[:, :lanes]
            rows_ref[j, 2 * f + 1 : 2 * f + 2, :] = kept[:, lanes:]
    for j in range(blk_count):
        message_ref[j] = jnp.concatenate([rows_ref[j], tail], 0).astype(jnp.bfloat16)


def synth_stage(values, factor, gains, sign, legendre_rows, blk_count):
    lanes, degree_count = values.shape
    rows = 2 * gains.shape[0]
    return pl.pallas_call(
        functools.partial(synth_kernel, blk_count),
        out_shape=jax.ShapeDtypeStruct((blk_count, 2 * rows, lanes), jnp.bfloat16),
        in_specs=[pl.BlockSpec(memory_space=pltpu.VMEM)] * 5,
        out_specs=pl.BlockSpec(memory_space=pltpu.VMEM),
        scratch_shapes=[
            pltpu.VMEM((2 * lanes, degree_count), jnp.bfloat16),
            pltpu.VMEM((blk_count, rows, lanes), jnp.float32),
        ],
        compiler_params=pltpu.CompilerParams(vmem_limit_bytes=14 << 20),
        name="synth_stage",
    )(values, factor, gains, sign, legendre_rows)


def adjoint_kernel(blk_count, returned_ref, gain_ref, sign_ref, legendre_ref, change_ref, left_ref):
    lanes, degree_count = change_ref.shape
    slot_count = lanes // 2
    funcs = gain_ref.shape[0]
    slot = lax.broadcasted_iota(jnp.int32, (slot_count, lanes), 0)
    lane = lax.broadcasted_iota(jnp.int32, (slot_count, lanes), 1)
    own = slot == lane % slot_count
    first = lax.broadcasted_iota(jnp.int32, (1, lanes), 1) < slot_count
    for a in range(blk_count // 2):
        near, far = returned_ref[2 * a], returned_ref[2 * a + 1]
        near_turned, far_turned = pltpu.roll(near, slot_count, 1), pltpu.roll(far, slot_count, 1)
        parts = (jnp.where(first, near, far_turned), jnp.where(first, near_turned, far))
        for c in range(2):
            for f in range(funcs):
                north = parts[c][2 * f : 2 * f + 1]
                south = parts[c][2 * f + 1 : 2 * f + 2]
                for u, hemis in enumerate((north + south, north - south)):
                    at = ((c * funcs + f) * 2 + u) * slot_count
                    left_ref[at : at + slot_count, a * lanes : (a + 1) * lanes] = jnp.where(
                        own, hemis, 0.0
                    ).astype(jnp.bfloat16)
    width = 256
    even_lane = lax.broadcasted_iota(jnp.int32, (slot_count, width), 1) % 2 == 0
    even_order = sign_ref[:slot_count, :] > 0.0
    even = even_lane == even_order
    for at in range(0, degree_count, width):
        parts = jnp.dot(
            left_ref[...], legendre_ref[:, at : at + width], preferred_element_type=jnp.float32
        )
        for c in range(2):
            total = None
            for f in range(funcs):
                base = (c * funcs + f) * 2 * slot_count
                picked = jnp.where(
                    even, parts[base : base + slot_count],
                    parts[base + slot_count : base + 2 * slot_count],
                )
                term = gain_ref[f : f + 1, at : at + width] * picked
                total = term if f == 0 else total + term
            change_ref[c * slot_count : (c + 1) * slot_count, at : at + width] = total


def adjoint_stage(returned, gains, sign, legendre_rows):
    blk_count, rows, lanes = returned.shape
    degree_count = legendre_rows.shape[1]
    return pl.pallas_call(
        functools.partial(adjoint_kernel, blk_count),
        out_shape=jax.ShapeDtypeStruct((lanes, degree_count), jnp.float32),
        in_specs=[pl.BlockSpec(memory_space=pltpu.VMEM)] * 4,
        out_specs=pl.BlockSpec(memory_space=pltpu.VMEM),
        scratch_shapes=[pltpu.VMEM((rows * lanes, legendre_rows.shape[0]), jnp.bfloat16)],
        compiler_params=pltpu.CompilerParams(vmem_limit_bytes=14 << 20),
        name="adjoint_stage",
    )(returned, gains, sign, legendre_rows)


def half_turn_sine(phase, quarter_turn):
    z = phase.astype(jnp.float32) * (1.0 / quarter_turn)
    y = z * z
    acc = jnp.float32(-3.41817280e-06)
    for coef in (1.60217136e-04, -4.68162024e-03, 7.96925873e-02, -6.45964093e-01, 1.57079633):
        acc = acc * y + jnp.float32(coef)
    return acc * z


def table_kernel(total, order_ref, table_ref):
    rows, half_lon = table_ref.shape
    slot_count = rows // total // 2
    period = 4 * half_lon * lax.axis_size("quarter")
    lane = lax.broadcasted_iota(jnp.int32, (slot_count, 128), 1)
    fine = (2 * lane + 1).astype(jnp.float32)
    coarse = (256 * jnp.minimum(lane, half_lon // 128)).astype(jnp.float32)

    def fill(d, carry):
        orders = order_ref[pl.ds(pl.multiple_of(d * slot_count, slot_count), slot_count), :]
        orders = orders.astype(jnp.float32)
        cos_b, sin_b = cos_sin((orders * fine).astype(jnp.int32), period)
        cos_a, sin_a = cos_sin((orders * coarse).astype(jnp.int32), period)
        at = pl.multiple_of(d * 2 * slot_count, 2 * slot_count)
        for i in range(half_lon // 128):
            cos_i, sin_i = cos_a[:, i : i + 1], sin_a[:, i : i + 1]
            lon = slice(i * 128, (i + 1) * 128)
            cosine = cos_i * cos_b - sin_i * sin_b
            sine = sin_i * cos_b + cos_i * sin_b
            table_ref[pl.ds(at, 2 * slot_count), lon] = jnp.concatenate([cosine, sine], 0).astype(
                jnp.bfloat16
            )
        return carry

    lax.fori_loop(0, total, fill, 0, unroll=4)


def table_stage(orders, total, half_lon):
    return pl.pallas_call(
        functools.partial(table_kernel, total),
        out_shape=jax.ShapeDtypeStruct((2 * orders.shape[0], half_lon), jnp.bfloat16),
        in_specs=[pl.BlockSpec(memory_space=pltpu.VMEM)],
        out_specs=pl.BlockSpec(memory_space=pltpu.VMEM),
        compiler_params=pltpu.CompilerParams(vmem_limit_bytes=14 << 20),
        name="table_stage",
    )(orders)


def cos_sin(steps, period):
    turn = jnp.bitwise_and(steps, period - 1)
    half = period // 2
    quarter = period // 4
    cosine = half_turn_sine(jnp.abs(turn - half) - quarter, quarter)
    shifted = jnp.bitwise_and(turn - quarter, period - 1)
    sine = half_turn_sine(jnp.abs(shifted - half) - quarter, quarter)
    return cosine, sine


def split_scalar(value, shape):
    hi = lax.reduce_precision(value, 8, 7)
    mid = lax.reduce_precision(value - hi, 8, 7)
    low = value - hi - mid
    lane = lax.broadcasted_iota(jnp.int32, shape, len(shape) - 1)
    zero = jnp.float32(0.0)
    picked = jnp.where(lane == 0, hi, jnp.where(lane == 1, mid, jnp.where(lane == 2, low, zero)))
    row = lax.broadcasted_iota(jnp.int32, shape, len(shape) - 2)
    return jnp.where(row == 0, picked, zero)


def body(start, observed, coverage, class_weight, degree_gain, legendre, order_table):
    blk_count = lax.axis_size("blk")
    quarter_count = lax.axis_size("quarter")
    blk_index = lax.axis_index("blk")
    quarter_index = lax.axis_index("quarter")
    total = blk_count * quarter_count
    slot_count, cycle_pairs, degree_count = legendre.shape
    order_count = order_table.shape[0]
    funcs, cycle_local, lon_local = observed.shape
    lon_total = lon_local * quarter_count
    half_lon = lon_local // 2
    rows = funcs * cycle_local
    lanes = 2 * slot_count
    pad_rows = -(rows + 1) % 16 + 1
    scale = lon_total ** (-0.5)
    bf16 = jnp.bfloat16
    first_slot = (blk_index * quarter_count + quarter_index) * slot_count
    my_orders = lax.dynamic_slice_in_dim(order_table, first_slot, slot_count)

    fused = lanes == 128 and rows == 8 and cycle_local == 2 and cycle_pairs == blk_count and half_lon % 128 == 0
    centre = 2 * lon_local * quarter_index + (lon_local - 1)
    cos_c, sin_c = cos_sin(order_table * centre, 2 * lon_total)
    if fused:
        table = table_stage(order_table[:, None], total, half_lon)
        cos_c = cos_c.reshape(total, 1, slot_count)
        sin_c = sin_c.reshape(total, 1, slot_count)
        cos_rot = jnp.concatenate([cos_c, cos_c], 2)
        sin_rot = jnp.concatenate([sin_c, -sin_c], 2)
    else:
        tile = min(128, half_lon)
        coarse = jnp.arange(half_lon // tile, dtype=jnp.int32) * tile
        fine = 2 * jnp.arange(tile, dtype=jnp.int32) + 1
        cos_a, sin_a = cos_sin(order_table[:, None] * (2 * coarse)[None, :], 2 * lon_total)
        cos_b, sin_b = cos_sin(order_table[:, None] * fine[None, :], 2 * lon_total)
        cos_a, sin_a, cos_b, sin_b, cos_c, sin_c = lax.optimization_barrier(
            (cos_a, sin_a, cos_b, sin_b, cos_c, sin_c)
        )
        cos_table = jnp.concatenate(
            [cos_a[:, i : i + 1] * cos_b - sin_a[:, i : i + 1] * sin_b for i in range(coarse.shape[0])], 1
        ).astype(bf16)
        sin_table = jnp.concatenate(
            [sin_a[:, i : i + 1] * cos_b + cos_a[:, i : i + 1] * sin_b for i in range(coarse.shape[0])], 1
        ).astype(bf16)

    pair_index = blk_index * (cycle_local // 2) + jnp.arange(cycle_local // 2, dtype=jnp.int32)
    theta = (pair_index.astype(jnp.float32) + 0.5) * (math.pi / (2 * cycle_pairs))
    area = jnp.repeat(jnp.sin(theta), 2)
    classes = jnp.arange(1, class_weight.shape[1] + 1, dtype=jnp.int32)
    matched = coverage[..., None] == classes
    cell_weight = jnp.sum(jnp.where(matched, class_weight[:, None, None, :], 0.0), -1)
    weight = (cell_weight * area[None, :, None]).reshape(rows, lon_local)

    def fold(grid):
        return grid[:, half_lon:], jnp.flip(grid[:, :half_lon], 1)

    observed_plus, observed_minus = fold(observed.reshape(rows, lon_local))
    weight_plus, weight_minus = fold(weight)
    precondition = 1.0 / (jnp.arange(degree_count, dtype=jnp.int32).astype(jnp.float32) + 1.0)

    degrees = jnp.arange(degree_count, dtype=jnp.int32)
    even_mask = ((degrees[None, :] + my_orders[:, None]) % 2 == 0)[:, None, None, :]

    def to_messages(coefficients, partial):
        scaled = degree_gain[None, :, None, :] * coefficients[:, None]
        zeros = jnp.zeros_like(scaled)
        parity = jnp.stack(
            [jnp.where(even_mask, scaled, zeros), jnp.where(even_mask, zeros, scaled)], 1
        ).astype(bf16)
        parts = jnp.einsum("sjl,stfcl->tjfcs", legendre, parity, preferred_element_type=jnp.float32)
        spectra = jnp.stack([parts[0] + parts[1], parts[0] - parts[1]], 1)
        spectra = spectra.reshape(blk_count, cycle_local, funcs, lanes).transpose(0, 2, 1, 3)
        spectra = spectra.reshape(blk_count, rows, lanes)
        tail = jnp.broadcast_to(split_scalar(partial, (pad_rows, lanes)), (blk_count, pad_rows, lanes))
        return jnp.concatenate([spectra, tail], 1).astype(bf16)

    def to_grid(coefficients, partial):
        messages = to_messages(coefficients, partial)
        arrived = exchange(messages, blk_count, quarter_count, True).astype(jnp.float32)
        summed = jnp.sum(arrived[:, rows:])
        spectra = arrived[:, :rows].reshape(total, rows, 2, slot_count).transpose(2, 1, 0, 3)
        spectra = spectra.reshape(2, rows, order_count)
        real = (spectra[0] * cos_c + spectra[1] * sin_c).astype(bf16)
        imag = (spectra[1] * cos_c - spectra[0] * sin_c).astype(bf16)
        even = scale * jnp.dot(real, cos_table, preferred_element_type=jnp.float32)
        odd = scale * jnp.dot(imag, sin_table, preferred_element_type=jnp.float32)
        return even + odd, even - odd, summed

    def to_orders(plus, minus, partial):
        contract = (((1,), (1,)), ((), ()))
        even = lax.dot_general(
            (plus + minus).astype(bf16), cos_table, contract, preferred_element_type=jnp.float32
        )
        odd = lax.dot_general(
            (plus - minus).astype(bf16), sin_table, contract, preferred_element_type=jnp.float32
        )
        real = scale * (even * cos_c - odd * sin_c)
        imag = scale * (even * sin_c + odd * cos_c)
        shares = jnp.stack([real, imag], 1).reshape(rows, 2, total, slot_count).transpose(2, 0, 1, 3)
        shares = shares.reshape(total, rows, lanes)
        tail = jnp.broadcast_to(split_scalar(partial, (pad_rows, lanes)), (total, pad_rows, lanes))
        messages = jnp.concatenate([shares, tail], 1).astype(bf16)
        arrived = exchange(messages, blk_count, quarter_count, False).astype(jnp.float32)
        summed = jnp.sum(arrived[:, rows:])
        returned = jnp.sum(arrived[:, :rows].reshape(blk_count, quarter_count, rows, lanes), 1)
        return to_coefficients(returned), summed

    def to_coefficients(returned):
        returned = returned.reshape(blk_count, funcs, cycle_local // 2, 2, 2, slot_count)
        north, south = returned[:, :, :, 0], returned[:, :, :, 1]
        combined = jnp.stack([north + south, north - south], 0).astype(bf16)
        combined = combined.transpose(5, 0, 4, 2, 1, 3).reshape(slot_count, 2, 2, funcs, cycle_pairs)
        parts = jnp.einsum("sjl,sucfj->sucfl", legendre, combined, preferred_element_type=jnp.float32)
        picked = jnp.where(even_mask, parts[:, 0], parts[:, 1])
        return jnp.sum(degree_gain[None, None, :, :] * picked, 2)

    zero = jnp.float32(0.0)
    one = jnp.float32(1.0)
    solution = start
    if fused:
        stacked_weight = jnp.concatenate([weight_plus, weight_minus], 0)
        image = jnp.concatenate([observed_plus, observed_minus], 0)
        legendre_rows = legendre.transpose(1, 0, 2).reshape(cycle_pairs * slot_count, degree_count)
        order_sign = (1 - 2 * (my_orders % 2)).astype(jnp.float32)
        order_sign = jnp.concatenate([order_sign, order_sign])[:, None]
        factor = precondition[None, :]

        def stage(factors, coefficients, multiplier, old):
            params = jnp.broadcast_to(jnp.stack(factors + [zero] * 4)[:, None], (8, lanes))
            messages = synth_stage(
                coefficients, multiplier, degree_gain, order_sign, legendre_rows, blk_count
            )
            returned, image, sums = grid_stage(
                params, messages, old, stacked_weight,
                cos_rot, sin_rot, table, blk_count, quarter_count, scale,
            )
            change = adjoint_stage(returned, degree_gain, order_sign, legendre_rows)
            return change, image, sums[0, 0], sums[1, 0]

        solution = start.transpose(1, 0, 2).reshape(lanes, degree_count)
        gradient, _, _, _ = stage([-one, one, zero, one], solution, jnp.ones_like(factor), image)
        direction = energy = None
        for iteration in range(ITERS):
            scaled_grad = factor * gradient
            factors = [one, zero, zero, one] if iteration == 0 else [one, zero, one, energy]
            change, image, energy_next, curvature = stage(factors, gradient, factor, image)
            if iteration == 0:
                direction = scaled_grad
            else:
                direction = scaled_grad + energy_next / energy * direction
            energy = energy_next
            step_size = energy / curvature
            solution = solution + step_size * direction
            gradient = gradient - step_size * change
        return tuple(
            out.reshape(2, slot_count, degree_count).transpose(1, 0, 2) for out in (solution, gradient)
        )
    plus, minus, _ = to_grid(start, zero)
    gradient, _ = to_orders(
        weight_plus * (observed_plus - plus), weight_minus * (observed_minus - minus), zero
    )
    direction = energy = image = None
    for iteration in range(ITERS):
        scaled_grad = precondition * gradient
        plus, minus, energy_next = to_grid(scaled_grad, jnp.sum(gradient * scaled_grad))
        if iteration == 0:
            direction = scaled_grad
        else:
            ratio = energy_next / energy
            direction = scaled_grad + ratio * direction
            plus = plus + ratio * image[0]
            minus = minus + ratio * image[1]
        image = (plus, minus)
        energy = energy_next
        weighted_plus, weighted_minus = weight_plus * plus, weight_minus * minus
        partial = jnp.sum(weighted_plus * plus + weighted_minus * minus)
        change, curvature = to_orders(weighted_plus, weighted_minus, partial)
        step_size = energy / curvature
        solution = solution + step_size * direction
        gradient = gradient - step_size * change
    return (solution, gradient)


def solution(mesh):
    return jax.shard_map(
        body,
        mesh=mesh,
        in_specs=(
            P(("blk", "quarter"), None, None),
            P(None, "blk", "quarter"),
            P(None, "blk", "quarter"),
            P(),
            P(),
            P(("blk", "quarter"), None, None),
            P(),
        ),
        out_specs=(P(("blk", "quarter"), None, None), P(("blk", "quarter"), None, None)),
        check_vma=False,
    )
```
